32 devices in a mesh: tm: 8 (over z, x), frac: 4 (over y, core).
Axes of the slice: x: 2, y: 2, z: 4, core: 2. Of those that a mesh axis runs over, the one named last changes fastest.
Arguments:
- pressure0: float32 [16, 32, 128], P('frac'), may hold values from -6 to 6
- storage: float32 [16, 32, 128], P('frac'), may hold values from 0.1 to 1
- perm_base: float32 [16, 32, 128], P('frac'), may hold values from 0.2 to 5
- leakoff: float32 [16, 32, 128], P('frac'), may hold values from 0.5 to 2
- sources: float32 [8, 16, 32, 128], P('tm', 'frac'), may hold values from -6 to 6
- export_cells: int32 [1024], P('frac'), may hold values from 0 to 16383
- inter_local: int32 [4096], P('frac'), may hold values from 0 to 16383
- trace_source: int32 [4096], P('frac'), may hold values from 0 to 1023, as said below
- inter_trans: float32 [4096], P('frac'), may hold values from 0.5 to 4
- inter_count: int32 [4], P('frac'), may hold values from 1 to 1024, 2048 in all
Outputs:
- slice_pressure: float32 [8, 16, 32, 128], P('tm', 'frac')
The draws below stay inside these ranges and needn't reach their ends.
Inputs may be any that keep to these rules, and one draw needn't show every extreme that they name: An entry of frac index d names a slot of another frac index: trace_source // 256 differs from d. `inter_count`: the live entries of a frac index are its first ones; the largest count is 1024.
All inputs are finite; a program needn't handle non-finite values. No bound on the sum of `inter_count` on one device may be relied on, other than what follows from the above.
Results may differ from the reference program's by a relative error of at most 0.00002.
Values sent between devices are 32-bit elements; how exact they have to be, the bound alone decides.
No kernel may reach another device: no remote copies, remote signals or barrier semaphores. Data moves between devices by JAX's collectives and lax.ppermute only.
A program may use at most 64 MiB of HBM per device.

```python
import math
import jax
import jax.numpy as jnp
import numpy as np
from jax import lax

F_DEV = 4
FROWS = 32
FCOLS = 128
FINE_STEPS = 4
SWEEPS = 8
COARSE_SWEEPS = 2
ITERS = 2
NE = 256
NI = 1024
CELLS_DEV = 16384
FRACS = 16
SLICES = 8
N_FRAC = 4


def draw_trace_source(key, part):
    total = N_FRAC * NI
    owner_key = jax.random.fold_in(key, 11)
    slot_key = jax.random.fold_in(key, 23)
    entry_index = jnp.arange(total, dtype=jnp.int32)
    home = entry_index // NI
    offset = jax.random.randint(owner_key, (total,), 1, N_FRAC, dtype=jnp.int32)
    owner = (home + offset) % N_FRAC
    within = jax.random.randint(slot_key, (total,), 0, NE, dtype=jnp.int32)
    return (owner * NE + within).astype(jnp.int32)


def with_ends(values, rng, least, top_value):
    index_at = [jax.random.randint(jax.random.fold_in(rng, axis), (), 0, length) for axis, length in enumerate(values.shape)]
    main_axis = values.shape.index(max(values.shape))
    neighbour = index_at[:main_axis] + [(index_at[main_axis] + 1) % values.shape[main_axis]] + index_at[main_axis + 1:]
    return values.at[tuple(index_at)].set(least).at[tuple(neighbour)].set(top_value)


def level_of(rng, extent, split, low, top_value):
    loudness, own = 1.0, jax.random.fold_in(rng, 6)
    for dim, shards_of in split:
        heights = jnp.exp(jax.random.uniform(jax.random.fold_in(own, dim), (shards_of,), jnp.float32, low / len(split), top_value / len(split)))
        loudness = loudness * jnp.repeat(heights, extent[dim] // shards_of).reshape([-1 if axis == dim else 1 for axis in range(len(extent))])
    return loudness


def length_profile(amount, total, limit, lean):
    portions = [(1 << 20) // math.isqrt(rank ** lean) + 1 for rank in range(2, amount + 1)]
    rest, holding = total - limit - (amount - 1), [1] * (amount - 1)
    while rest > 0:
        movable = [i for i in range(amount - 1) if holding[i] < limit]
        pool, remaining = sum([portions[i] for i in movable]), rest
        for i in movable:
            more = min(limit - holding[i], max(1, remaining * portions[i] // pool), rest)
            holding[i] = holding[i] + more
            rest = rest - more
    return np.array([limit] + holding)


def uneven(stream_key, number_of, total, limit, skew):
    if number_of == 2:
        one = jax.random.randint(stream_key, (), max(1, total - limit), min(limit, total - 1) + 1)
        return jnp.stack([one, total - one])
    tallies = jnp.asarray(length_profile(number_of, total, limit, skew), jnp.int32)
    pairs = (number_of - 1) // 2
    source_of, sink = tallies[1:1 + 2 * pairs:2], tallies[2:2 + 2 * pairs:2]
    margin = jnp.minimum(source_of - 1, limit - sink)
    passed = jax.random.randint(jax.random.fold_in(stream_key, 1), (pairs,), 0, 1 << 20) % (margin + 1)
    tallies = tallies.at[1:1 + 2 * pairs:2].set(source_of - passed).at[2:2 + 2 * pairs:2].set(sink + passed)
    return tallies[jax.random.permutation(jax.random.fold_in(stream_key, 2), number_of)]


def bell_draw(rng, extent, scale, reach, cuts=(), held_as=jnp.bfloat16):
    values = scale * jax.random.normal(rng, extent, jnp.float32)
    if cuts:
        values = values * level_of(rng, extent, cuts, -0.22, 0.18)
    return jnp.clip(values, -reach, reach).astype(held_as)


def setup_inputs(seed: int = 0) -> dict:
    key_list = jax.random.split(jax.random.key(seed), 11)
    return {
        "pressure0": bell_draw(key_list[0], (FRACS, FROWS, FCOLS), 1.0, 6.0, ((0, 4),), jnp.float32),
        "storage": jnp.clip(jnp.exp(math.log(1.0) - 2.3025851 * jax.random.uniform(key_list[1], (FRACS, FROWS, FCOLS), jnp.float32) ** level_of(key_list[1], (FRACS, FROWS, FCOLS), ((0, 4),), -0.2, 0.2)), 0.1, 1.0),
        "perm_base": jnp.clip(jnp.exp(math.log(5.0) - 3.218876 * jax.random.uniform(key_list[2], (FRACS, FROWS, FCOLS), jnp.float32) ** level_of(key_list[2], (FRACS, FROWS, FCOLS), ((0, 4),), -0.2, 0.2)), 0.2, 5.0),
        "leakoff": jnp.clip(jnp.exp(math.log(2.0) - 1.3862944 * jax.random.uniform(key_list[3], (FRACS, FROWS, FCOLS), jnp.float32) ** level_of(key_list[3], (FRACS, FROWS, FCOLS), ((0, 4),), -0.2, 0.2)), 0.5, 2.0),
        "sources": bell_draw(key_list[4], (SLICES, FRACS, FROWS, FCOLS), 1.0, 6.0, ((0, 8), (1, 4)), jnp.float32),
        "export_cells": with_ends(jax.random.randint(key_list[5], (N_FRAC * NE,), 0, CELLS_DEV), jax.random.fold_in(key_list[5], 1), 0, CELLS_DEV - 1).astype(jnp.int32),
        "inter_local": with_ends(jax.random.randint(key_list[6], (N_FRAC * NI,), 0, CELLS_DEV), jax.random.fold_in(key_list[6], 1), 0, CELLS_DEV - 1).astype(jnp.int32),
        "trace_source": draw_trace_source(jax.random.fold_in(key_list[10], 71), 0),
        "inter_trans": jnp.clip(jnp.exp(math.log(4.0) - 2.0794415 * jax.random.uniform(key_list[8], (N_FRAC * NI,), jnp.float32) ** level_of(key_list[8], (N_FRAC * NI,), ((0, 4),), -0.2, 0.2)), 0.5, 4.0),
        "inter_count": uneven(key_list[9], N_FRAC, N_FRAC * NI // 2, NI, 2).astype(jnp.int32),
    }


stress_factor = 0.15
fine_size = 0.25


def next_rows(array):
    return jnp.concatenate([array[:, 1:, :], jnp.zeros_like(array[:, :1, :])], axis=1)


def prev_rows(array):
    return jnp.concatenate([jnp.zeros_like(array[:, :1, :]), array[:, :-1, :]], axis=1)


def next_cols(array):
    return jnp.concatenate([array[:, :, 1:], jnp.zeros_like(array[:, :, :1])], axis=2)


def prev_cols(array):
    return jnp.concatenate([jnp.zeros_like(array[:, :, :1]), array[:, :, :-1]], axis=2)


def implicit(pressure, slice_source, step_size, sweeps, fields, couple):
    storage, perm_base, leakoff, tisum = fields
    permeability = perm_base * jnp.exp(stress_factor * pressure)
    row_index = lax.broadcasted_iota(jnp.int32, pressure.shape, 1)
    col_index = lax.broadcasted_iota(jnp.int32, pressure.shape, 2)
    face_rows = jnp.where(row_index < pressure.shape[1] - 1, 0.5 * (permeability + next_rows(permeability)), 0.0)
    face_cols = jnp.where(col_index < pressure.shape[2] - 1, 0.5 * (permeability + next_cols(permeability)), 0.0)
    storage_rate = storage / step_size
    diagonal_total = storage_rate + leakoff + face_rows + prev_rows(face_rows) + face_cols + prev_cols(face_cols)
    right_side = storage_rate * pressure + slice_source
    if couple is not None:
        diagonal_total = diagonal_total + tisum
        right_side = right_side + couple(pressure)

    def sweep(sweep_index, current):
        beside = face_rows * next_rows(current) + prev_rows(face_rows * current)
        beside = beside + face_cols * next_cols(current) + prev_cols(face_cols * current)
        return (right_side + beside) / diagonal_total

    return lax.fori_loop(0, sweeps, sweep, pressure)


def reference(pressure0, storage, perm_base, leakoff, sources, export_cells, inter_local, trace_source, inter_trans, inter_count):
    cells = F_DEV * FROWS * FCOLS
    slot_index = jnp.arange(N_FRAC * NE, dtype=jnp.int32)
    export_global = (slot_index // NE) * cells + export_cells
    remote_cell = export_global[trace_source]
    entry_index = jnp.arange(N_FRAC * NI, dtype=jnp.int32)
    local_cell = (entry_index // NI) * cells + inter_local
    live_entry = (entry_index % NI) < inter_count[entry_index // NI]
    weights = jnp.where(live_entry, inter_trans, jnp.zeros_like(inter_trans))
    tisum = jnp.zeros((FRACS * FROWS * FCOLS,), inter_trans.dtype).at[local_cell].add(weights).reshape(pressure0.shape)
    fields = (storage, perm_base, leakoff, tisum)

    def couple(current):
        flat_field = current.reshape(-1)
        remote_values = flat_field[remote_cell]
        return jnp.zeros_like(flat_field).at[local_cell].add(weights * remote_values).reshape(current.shape)

    def coarse(pressure, slice_source):
        return implicit(pressure, slice_source, fine_size * FINE_STEPS, COARSE_SWEEPS, fields, None)

    def fine(pressure, slice_source):
        for step_number in range(FINE_STEPS):
            pressure = implicit(pressure, slice_source, fine_size, SWEEPS, fields, couple)
        return pressure

    def chain(deltas):
        def advance(current, inputs):
            slice_source, correction = inputs
            following = coarse(current, slice_source) + correction
            return following, following

        final_state, states = lax.scan(advance, pressure0, (sources[:-1], deltas))
        return jnp.concatenate([pressure0[None], states], axis=0)

    states = chain(jnp.zeros_like(sources[:-1]))
    for iteration in range(ITERS):
        fine_ends = lax.map(lambda pair: fine(pair[0], pair[1]), (states[:-1], sources[:-1]))
        coarse_ends = lax.map(lambda pair: coarse(pair[0], pair[1]), (states[:-1], sources[:-1]))
        states = chain(fine_ends - coarse_ends)
    return states
```

```python
import functools
import math

import jax
import jax.numpy as jnp
from jax import lax
from jax.experimental import pallas as pl
from jax.experimental.pallas import tpu as pltpu
from jax.sharding import Mesh, PartitionSpec as P

FINE_STEPS = 4
SWEEPS = 8
COARSE_SWEEPS = 2
ITERS = 2

stress_factor = 0.15
fine_size = 0.25

LANES = 128
SUBS = 8
CHUNK = 256
F32 = jnp.float32
BF16 = jnp.bfloat16
VMEM = pl.BlockSpec(memory_space=pltpu.VMEM)
HBM = pl.BlockSpec(memory_space=pltpu.HBM)
SMEM = pl.BlockSpec(memory_space=pltpu.SMEM)


def shape_of(*dims, dtype=F32):
    return jax.ShapeDtypeStruct(dims, dtype)


def call(kernel, name, args, outs, scratch=(), specs=None):
    size = sum(math.prod(a.shape) * a.dtype.itemsize for a in (*args, *outs))
    return pl.pallas_call(
        kernel,
        out_shape=outs,
        in_specs=specs or [VMEM] * len(args),
        out_specs=(VMEM,) * len(outs),
        scratch_shapes=scratch,
        compiler_params=pltpu.CompilerParams(vmem_limit_bytes=12 * 2**20 + 2 * size),
        name=name,
    )(*args)


def lane_roll(x, s):
    return pltpu.roll(x, s % LANES, axis=2)


def sub_roll(x, s):
    return pltpu.roll(x, s % SUBS, axis=1)


def implicit(q, s, c, sto, per, lea, tis, step_size, sweeps):
    J = len(q)
    shape = q[0].shape
    row = lax.broadcasted_iota(jnp.int32, shape, 1)
    col = lax.broadcasted_iota(jnp.int32, shape, 2)
    first_row, last_row, first_col, last_col = row == 0, row == SUBS - 1, col == 0, col == LANES - 1
    k = [(0.5 * per[j]) * jnp.exp(stress_factor * q[j]) for j in range(J)]
    row_next = [k[j] + k[j + 1] for j in range(J - 1)]
    edge = jnp.where(last_row, 0.0, k[J - 1] + sub_roll(k[0], -1))
    row_prev = [jnp.where(first_row, 0.0, k[0] + sub_roll(k[J - 1], 1))] + row_next
    row_next = row_next + [edge]
    col_next = [jnp.where(last_col, 0.0, k[j] + lane_roll(k[j], -1)) for j in range(J)]
    col_prev = [jnp.where(first_col, 0.0, k[j] + lane_roll(k[j], 1)) for j in range(J)]
    rhs, a_rn, a_rp, a_cn, a_cp = [], [], [], [], []
    for j in range(J):
        rate = sto[j] * (1.0 / step_size)
        total = rate + lea[j]
        b = rate * q[j] + s[j]
        if tis is not None:
            total = total + tis[j]
            b = b + c[j]
        inv = 1.0 / ((total + (row_next[j] + row_prev[j])) + (col_next[j] + col_prev[j]))
        rhs.append(b * inv)
        a_rn.append(row_next[j] * inv)
        a_rp.append(row_prev[j] * inv)
        a_cn.append(col_next[j] * inv)
        a_cp.append(col_prev[j] * inv)
    v = q
    for _ in range(sweeps):
        down = v[1:] + [sub_roll(v[0], -1)]
        up = [sub_roll(v[J - 1], 1)] + v[:-1]
        v = [
            (rhs[j] + a_rn[j] * down[j])
            + (a_rp[j] * up[j] + (a_cn[j] * lane_roll(v[j], -1) + a_cp[j] * lane_roll(v[j], 1)))
            for j in range(J)
        ]
    return v


def rows_of(ref, index, J):
    return [ref[(*index, pl.ds(j, SUBS, stride=J), slice(None))] for j in range(J)]


def put_rows(ref, index, J, parts):
    for j in range(J):
        ref[(*index, pl.ds(j, SUBS, stride=J), slice(None))] = parts[j]


def split_high_low(x, pieces):
    out = []
    for _ in range(pieces):
        part = x.astype(BF16).astype(F32)
        out.append(part)
        x = x - part
    return out


def scatter_rows(values, rt_ref, l_ref, d):
    rows = rt_ref.shape[1]
    entries = rt_ref.shape[2]
    total = jnp.zeros((len(values) * rows, LANES), F32)
    for g in range(entries // CHUNK):
        pieces = []
        for value in values:
            cols = []
            for m in range(g * CHUNK // LANES, (g + 1) * CHUNK // LANES):
                row = jnp.broadcast_to(value[m : m + 1, :], (rows, LANES)).astype(BF16)
                cols.append(rt_ref[d, :, m * LANES : (m + 1) * LANES] * row)
            pieces.append(jnp.concatenate(cols, axis=1))
        a = jnp.concatenate(pieces, axis=0)
        total = total + jnp.dot(
            a, l_ref[d, g * CHUNK : (g + 1) * CHUNK, :], preferred_element_type=F32
        )
    out = total[:rows]
    for i in range(1, len(values)):
        out = out + total[i * rows : (i + 1) * rows]
    return out


class Layout:
    def __init__(self, held, frac_rows, entries, exports):
        self.held, self.frac_rows = held, frac_rows
        self.entry_rows = entries // LANES
        self.export_rows = exports // LANES
        padded = -(-self.export_rows // SUBS) * SUBS
        self.starts = [k * self.entry_rows for k in range(4)]
        self.sizes = [self.entry_rows] * 3 + [self.export_rows]
        self.slots = 3 * held + -(-(3 * self.entry_rows + padded) // frac_rows)

    def places(self, kind):
        at, left = self.starts[kind], self.sizes[kind]
        while left:
            n = min(left, SUBS)
            yield 3 * self.held + at // self.frac_rows, at % self.frac_rows, n
            at, left = at + n, left - n

    def entries(self, ref, d, kind):
        parts = [ref[d, slot, r : r + n, :] for slot, r, n in self.places(kind)]
        return parts[0] if len(parts) == 1 else jnp.concatenate(parts, axis=0)

    def put(self, ref, kind, value):
        at = 0
        for slot, r, n in self.places(kind):
            ref[slot, r : r + n, :] = value[at : at + n]
            at += n


def pack_kernel(layout, count_ref, sto, per, lea, loc, trace, w, exp, blocks_ref, out_ref, loc_v, trace_v, w_v, exp_v, sems):
    held = layout.held
    copies = [(a, out_ref.at[pl.ds(k * held, held)]) for k, a in enumerate((sto, per, lea))]
    copies += [(loc, loc_v), (trace, trace_v), (w, w_v), (exp, exp_v)]
    copies = [pltpu.make_async_copy(a, b, sems.at[k]) for k, (a, b) in enumerate(copies)]
    for c in copies:
        c.start()
    out_ref[3 * held :] = jnp.zeros((layout.slots - 3 * held, *out_ref.shape[1:]), F32)
    for c in copies:
        c.wait()
    shape = w_v.shape
    index = lax.broadcasted_iota(jnp.int32, shape, 0) * LANES + lax.broadcasted_iota(jnp.int32, shape, 1)
    layout.put(out_ref, 0, loc_v[...].astype(F32))
    layout.put(out_ref, 1, trace_v[...].astype(F32))
    layout.put(out_ref, 2, jnp.where(index < count_ref[0], w_v[...], 0.0))
    layout.put(out_ref, 3, exp_v[...].astype(F32))


def prep_kernel(layout, *refs):
    *piece_refs, st_ref, rt_ref, l_ref, tis_ref = refs
    parts, rows, entries = rt_ref.shape
    me = lax.axis_index("frac")
    for k in range(parts):
        st_ref[lax.rem(me - k + parts, parts)] = piece_refs[k][...]
    for d in range(parts):
        cell = layout.entries(st_ref, d, 0).astype(jnp.int32)
        row, col = cell // LANES, cell % LANES
        for m in range(entries // LANES):
            at = slice(m * LANES, (m + 1) * LANES)
            iota_r = lax.broadcasted_iota(jnp.int32, (rows, LANES), 0)
            iota_l = lax.broadcasted_iota(jnp.int32, (LANES, LANES), 0)
            rt_ref[d, :, at] = jnp.where(iota_r == row[m : m + 1, :], 1.0, 0.0).astype(BF16)
            lt = jnp.where(iota_l == col[m : m + 1, :], 1.0, 0.0)
            l_ref[d, at, :] = lt.T.astype(BF16)
        tis = scatter_rows(split_high_low(layout.entries(st_ref, d, 2), 3), rt_ref, l_ref, d)
        per_part = tis_ref.shape[0] // parts
        tis_ref[d * per_part : (d + 1) * per_part] = tis.reshape(per_part, *tis_ref.shape[1:])


def couple(o_ref, c_ref, st_ref, layout, rt_ref, l_ref):
    parts, rows, _ = rt_ref.shape
    frac_rows = o_ref.shape[1]
    per_part = rows // frac_rows
    export_rows = layout.export_rows
    iota = lax.broadcasted_iota(jnp.int32, (SUBS, LANES), 0)
    exported = []
    for d in range(parts):
        cell = layout.entries(st_ref, d, 3).astype(jnp.int32)
        for e in range(export_rows):
            at = jnp.broadcast_to(cell[e : e + 1, :], (SUBS, LANES))
            row, col = at // LANES - iota, at % LANES
            found = [jnp.zeros((SUBS, LANES), F32) for _ in range(2)]
            for t in range(rows // SUBS):
                f, r = d * per_part + t * SUBS // frac_rows, t * SUBS % frac_rows
                got = jnp.take_along_axis(
                    o_ref[f, r : r + SUBS, :], col, axis=1, mode="promise_in_bounds"
                )
                found[t % 2] = jnp.where(row == t * SUBS, got, found[t % 2])
            exported.append(jnp.sum(found[0] + found[1], axis=0, keepdims=True))
    for d in range(parts):
        slot = layout.entries(st_ref, d, 1).astype(jnp.int32)
        row, col = slot // LANES, slot % LANES
        x = jnp.zeros(slot.shape, F32)
        for t in range(parts * export_rows):
            got = jnp.take_along_axis(
                jnp.broadcast_to(exported[t], slot.shape), col, axis=1, mode="promise_in_bounds"
            )
            x = jnp.where(row == t, got, x)
        c = scatter_rows(split_high_low(layout.entries(st_ref, d, 2) * x, 2), rt_ref, l_ref, d)
        c_ref[d * per_part : (d + 1) * per_part] = c.reshape(per_part, *o_ref.shape[1:])


def fine_kernel(layout, u_ref, s_ref, st_ref, tis_ref, rt_ref, l_ref, o_ref, c_ref):
    total = o_ref.shape[0]
    held = layout.held
    group = math.gcd(total, 16)
    J = o_ref.shape[1] // SUBS
    own = s_ref.shape[2]
    o_ref[...] = (u_ref[:, 0] if len(u_ref.shape) == 5 else u_ref[...]).reshape(o_ref.shape)

    def step(_, carry):
        couple(o_ref, c_ref, st_ref, layout, rt_ref, l_ref)

        def turn(g, carry):
            at = (pl.ds(g * group, group),)
            q, c, tis = (rows_of(ref, at, J) for ref in (o_ref, c_ref, tis_ref))
            flat = lambda parts: [x.reshape(q[0].shape) for x in parts]
            n = group // held
            sto, per, lea = (
                flat(rows_of(st_ref, (pl.ds(g * n, n), slice(k * held, (k + 1) * held)), J)) for k in range(3)
            )
            n = group // own
            s = flat(rows_of(s_ref, (pl.ds(g * n, n), 1, slice(None)), J))
            put_rows(o_ref, at, J, implicit(q, s, c, sto, per, lea, tis, fine_size, SWEEPS))
            return carry

        return lax.fori_loop(0, total // group, turn, carry)

    lax.fori_loop(0, FINE_STEPS, step, 0)


def chain_kernel(layout, kind, *refs):
    if kind == 0:
        p_ref, field_ref, s_ref, u_ref = refs
    elif kind == 1:
        p_ref, field_ref, s_ref, f_ref, old_ref, u_ref, g_ref = refs
    else:
        p_ref, field_ref, s_ref, f_ref, old_ref, out_ref, u_ref = refs
    slices, own = s_ref.shape[:2]
    J = p_ref.shape[1] // SUBS
    held, inner = layout.held, layout.held // own
    x = lax.axis_index("x")
    all_own = slice(None)
    sto, per, lea = (rows_of(field_ref, (pl.ds(k * held + x * own, own),), J) for k in range(3))
    at = (lambda n: (n, 0, all_own)) if kind == 0 else (lambda n: (n, all_own))
    start = rows_of(p_ref, (pl.ds(x * own, own),), J)
    put_rows(u_ref, at(0), J, start)
    if kind == 0:
        u_ref[:, 1] = s_ref[...]

    def turn(n, u):
        s = rows_of(s_ref, (n, all_own), J)
        g = implicit(list(u), s, None, sto, per, lea, None, fine_size * FINE_STEPS, COARSE_SWEEPS)
        if kind:
            f = rows_of(f_ref, (n, all_own), J)
            old = rows_of(old_ref, (n + 1, 0, all_own) if len(old_ref.shape) == 5 else (n, all_own), J)
            if kind == 1:
                put_rows(g_ref, (n, all_own), J, g)
            g = [g[j] + (f[j] - old[j]) for j in range(J)]
        put_rows(u_ref, at(n + 1), J, g)
        return tuple(g)

    lax.fori_loop(0, slices - 1, turn, tuple(start))
    if kind == 1:
        g_ref[slices - 1] = jnp.zeros(g_ref.shape[1:], F32)
    if kind == 2:
        z = lax.axis_index("z")
        for k in range(inner):
            out_ref[k] = u_ref[z * inner + lax.rem(x + k, inner)]


def body(sizes, pressure0, storage, perm_base, leakoff, sources, export_cells, inter_local, trace_source, inter_trans, inter_count):
    groups, inner, fracs = sizes
    slices = groups * inner
    held, frac_rows, _ = pressure0.shape
    own = held // inner
    plane = ("frac", "x")
    layout = Layout(held, frac_rows, inter_local.size, export_cells.size)
    block = (own, frac_rows, LANES)

    blocks = jnp.broadcast_to(sources[0].reshape(1, inner, *block), (groups, inner, *block)).reshape(slices, *block)
    own_sources = lax.all_to_all(blocks, ("z", "x"), 0, 0, tiled=True)

    lists = [a.reshape(-1, LANES) for a in (inter_local, trace_source, inter_trans, export_cells)]
    (packed,) = call(
        functools.partial(pack_kernel, layout),
        "pack",
        (inter_count, storage, perm_base, leakoff, *lists, blocks),
        (shape_of(layout.slots, frac_rows, LANES),),
        [pltpu.VMEM(a.shape, a.dtype) for a in lists] + [pltpu.SemaphoreType.DMA((7,))],
        [SMEM] + [HBM] * 7 + [pl.BlockSpec(memory_space=pl.ANY)],
    )
    pieces = [packed] + [
        lax.ppermute(packed, "frac", [(i, (i + k) % fracs) for i in range(fracs)]) for k in range(1, fracs)
    ]
    own_sources, *pieces = lax.optimization_barrier((own_sources, *pieces))
    cells = held * frac_rows
    st, rt, l, tis = call(
        functools.partial(prep_kernel, layout),
        "prep",
        pieces,
        (
            shape_of(fracs, *packed.shape),
            shape_of(fracs, cells, inter_local.size, dtype=BF16),
            shape_of(fracs, inter_local.size, LANES, dtype=BF16),
            shape_of(fracs * held, frac_rows, LANES),
        ),
    )

    base = (pressure0, packed, own_sources)
    (u0,) = call(functools.partial(chain_kernel, layout, 0), "chain0", base, (shape_of(slices, 2, *block),))
    b0 = lax.all_to_all(u0, plane, 0, 0, tiled=True)
    u, old = b0, u0
    plain = shape_of(slices, *block)
    whole = (fracs * held, frac_rows, LANES)
    for iteration in range(ITERS):
        (ends,) = call(
            functools.partial(fine_kernel, layout),
            "fine",
            (u, b0, st, tis, rt, l),
            (shape_of(*whole),),
            [pltpu.VMEM(whole, F32)],
        )
        ends = lax.all_to_all(ends.reshape(plain.shape), plane, 0, 0, tiled=True)
        if iteration < ITERS - 1:
            states, old = call(functools.partial(chain_kernel, layout, 1), "chain1", (*base, ends, old), (plain, plain))
            u = lax.all_to_all(states, plane, 0, 0, tiled=True)
    (mine,) = call(
        functools.partial(chain_kernel, layout, 2),
        "chain2",
        (*base, ends, old),
        (shape_of(inner, *block),),
        [pltpu.VMEM(plain.shape, F32)],
    )
    x = lax.axis_index("x")
    got = [mine[0]] + [
        lax.ppermute(mine[k], "x", [(i, (i + k) % inner) for i in range(inner)]) for k in range(1, inner)
    ]
    return jnp.stack([lax.select_n((x - i) % inner, *got) if inner > 2 else jnp.where(x == i, got[0], got[-1]) for i in range(inner)]).reshape(1, held, frac_rows, LANES)


def solution(mesh):
    slices, fracs = mesh.shape["tm"], mesh.shape["frac"]
    inner = slices // fracs
    sizes = (slices // inner, inner, fracs)
    mesh = Mesh(mesh.devices.reshape(sizes), ("z", "x", "frac"))
    frac = P("frac")
    both = P(("z", "x"), "frac")
    return jax.shard_map(
        functools.partial(body, sizes),
        mesh=mesh,
        in_specs=(frac,) * 4 + (both,) + (frac,) * 5,
        out_specs=both,
        check_vma=False,
    )
```

```python
import functools
import math

import jax
import jax.numpy as jnp
from jax import lax
from jax.experimental import pallas as pl
from jax.experimental.pallas import tpu as pltpu
from jax.sharding import Mesh, PartitionSpec as P

FINE_STEPS = 4
SWEEPS = 8
COARSE_SWEEPS = 2
ITERS = 2

stress_factor = 0.15
fine_size = 0.25

LANES = 128
SUBS = 8
F32 = jnp.float32
BF16 = jnp.bfloat16
VMEM = pl.BlockSpec(memory_space=pltpu.VMEM)
HBM = pl.BlockSpec(memory_space=pltpu.HBM)


def shape_of(*dims, dtype=F32):
    return jax.ShapeDtypeStruct(dims, dtype)


def call(kernel, name, args, outs, scratch=(), specs=None, room=4 * 2**20):
    size = sum(math.prod(a.shape) * a.dtype.itemsize for a in (*args, *outs))
    return pl.pallas_call(
        kernel,
        out_shape=outs,
        in_specs=specs or [VMEM] * len(args),
        out_specs=(VMEM,) * len(outs),
        scratch_shapes=scratch,
        compiler_params=pltpu.CompilerParams(vmem_limit_bytes=room + size),
        name=name,
    )(*args)


def lane_roll(x, s):
    return pltpu.roll(x, s % LANES, axis=2)


def sub_roll(x, s):
    return pltpu.roll(x, s % SUBS, axis=1)


def columns_after(v):
    return v[1:] + [[lane_roll(x, -1) for x in v[0]]]


def columns_before(v):
    return [[lane_roll(x, 1) for x in v[-1]]] + v[:-1]


def rows_after(v):
    return [part[1:] + [sub_roll(part[0], -1)] for part in v]


def rows_before(v):
    return [[sub_roll(part[-1], 1)] + part[:-1] for part in v]


def implicit(q, s, c, sto, per, lea, tis, step_size, sweeps):
    M, J = len(q), len(q[0])
    shape = q[0][0].shape
    row = lax.broadcasted_iota(jnp.int32, shape, 1)
    col = lax.broadcasted_iota(jnp.int32, shape, 2) % (LANES // M)
    grid = [(k, j) for k in range(M) for j in range(J)]

    def each(f):
        return [[f(k, j) for j in range(J)] for k in range(M)]

    half = each(lambda k, j: (0.5 * per[k][j]) * jnp.exp(stress_factor * q[k][j]))
    down, up, right, left = rows_after(half), rows_before(half), columns_after(half), columns_before(half)
    row_next = each(lambda k, j: half[k][j] + down[k][j])
    row_prev = each(lambda k, j: half[k][j] + up[k][j] if j == 0 else row_next[k][j - 1])
    col_next = each(lambda k, j: half[k][j] + right[k][j])
    col_prev = each(lambda k, j: half[k][j] + left[k][j] if k == 0 else col_next[k - 1][j])
    for k in range(M):
        row_next[k][J - 1] = jnp.where(row == SUBS - 1, 0.0, row_next[k][J - 1])
        row_prev[k][0] = jnp.where(row == 0, 0.0, row_prev[k][0])
    for j in range(J):
        col_next[M - 1][j] = jnp.where(col == LANES // M - 1, 0.0, col_next[M - 1][j])
        col_prev[0][j] = jnp.where(col == 0, 0.0, col_prev[0][j])
    rhs, a_rn, a_rp, a_cn, a_cp = (each(lambda k, j: None) for _ in range(5))
    for k, j in grid:
        rate = sto[k][j] * (1.0 / step_size)
        total = rate + lea[k][j]
        b = rate * q[k][j] + s[k][j]
        if tis is not None:
            total = total + tis[k][j]
            b = b + c[k][j]
        inv = 1.0 / ((total + (row_next[k][j] + row_prev[k][j])) + (col_next[k][j] + col_prev[k][j]))
        rhs[k][j] = b * inv
        a_rn[k][j] = row_next[k][j] * inv
        a_rp[k][j] = row_prev[k][j] * inv
        a_cn[k][j] = col_next[k][j] * inv
        a_cp[k][j] = col_prev[k][j] * inv
    v = q
    for _ in range(sweeps):
        down, up, right, left = rows_after(v), rows_before(v), columns_after(v), columns_before(v)
        v = each(
            lambda k, j: (rhs[k][j] + a_rn[k][j] * down[k][j] + a_rp[k][j] * up[k][j])
            + (a_cn[k][j] * right[k][j] + a_cp[k][j] * left[k][j])
        )
    return v


def parts_of(ref, index, first, M, J):
    return [[ref[(*index, first + k, pl.ds(j * SUBS, SUBS), slice(None))] for j in range(J)] for k in range(M)]


def put_parts(ref, index, first, parts):
    for k, part in enumerate(parts):
        for j, x in enumerate(part):
            ref[(*index, first + k, pl.ds(j * SUBS, SUBS), slice(None))] = x


def pick_lanes(x, index):
    return jnp.take_along_axis(x, index, axis=1, mode="promise_in_bounds")


def to_parts(ref, first, M, J):
    lane = lax.broadcasted_iota(jnp.int32, (SUBS, LANES), 1)
    width = LANES // M
    out = [[None] * J for _ in range(M)]
    for j in range(J):
        rows = [ref[first + f, pl.ds(j, SUBS, stride=J), :] for f in range(M)]
        for k in range(M):
            x = pick_lanes(rows[0], lane % width * M + k)
            for f in range(1, M):
                x = jnp.where(lane // width == f, pick_lanes(rows[f], lane % width * M + k), x)
            out[k][j] = x
    return out


def from_parts(ref, index, parts):
    lane = lax.broadcasted_iota(jnp.int32, (SUBS, LANES), 1)
    M, J = len(parts), len(parts[0])
    width = LANES // M
    for j in range(J):
        for f in range(M):
            x = pick_lanes(parts[0][j], lane // M + f * width)
            for k in range(1, M):
                x = jnp.where(lane % M == k, pick_lanes(parts[k][j], lane // M + f * width), x)
            ref[(*index, f, pl.ds(j, SUBS, stride=J), slice(None))] = x


def split_high_low(x, pieces):
    out = []
    for _ in range(pieces):
        part = x.astype(BF16).astype(F32)
        out.append(part)
        x = x - part
    return out


def scatter_rows(values, rt_ref, l_ref, d):
    rows, entries = rt_ref.shape[1:]
    pieces = []
    for value in values:
        cols = []
        for m in range(entries // LANES):
            row = jnp.broadcast_to(value[m : m + 1, :], (2 * SUBS, LANES)).astype(BF16)
            hot = rt_ref[d, :, m * LANES : (m + 1) * LANES].reshape(-1, 2 * SUBS, LANES)
            cols.append((hot * row[None]).reshape(rows, LANES))
        pieces.append(jnp.concatenate(cols, axis=1))
    both = jnp.dot(jnp.concatenate(pieces, axis=0), l_ref[d], preferred_element_type=F32)
    out = both[:rows]
    for i in range(1, len(values)):
        out = out + both[i * rows : (i + 1) * rows]
    return jnp.concatenate([out[:, h * LANES : (h + 1) * LANES] for h in range(out.shape[1] // LANES)], axis=0)


class Layout:
    def __init__(self, held, own, pair, frac_rows, entries, exports):
        self.held, self.own, self.pair, self.frac_rows = held, own, pair, frac_rows
        self.J = frac_rows // SUBS
        self.entry_rows = entries // LANES
        self.export_rows = exports // LANES
        padded = -(-self.export_rows // SUBS) * SUBS
        self.sizes = [self.entry_rows] * 3 + [self.export_rows]
        self.slots = 3 * held + -(-(3 * self.entry_rows + padded) // frac_rows)

    def place(self, cell):
        own, J = self.own, self.J
        f, row, col = cell // (self.frac_rows * LANES), cell // LANES % self.frac_rows, cell % LANES
        part = (f // own * own + col % own) * J + row % J
        return (part * SUBS + row // J) * LANES + f % own * (LANES // own) + col // own

    def entries(self, ref, d, kind):
        start = kind * self.entry_rows
        return ref[d, start : start + self.sizes[kind], :]

    def put(self, ref, kind, value):
        at, left, start = 0, self.sizes[kind], kind * self.entry_rows
        while left:
            n = min(left, SUBS)
            slot, r = 3 * self.held + start // self.frac_rows, start % self.frac_rows
            ref[slot, r : r + n, :] = value[at : at + n]
            at, start, left = at + n, start + n, left - n


def pack_kernel(layout, *refs):
    sources = refs[:10]
    out_ref, blocks_ref, p_ref = refs[10:13]
    held_refs, sems = refs[13:23], refs[23]
    held, own, J = layout.held, layout.own, layout.J
    copies = [pltpu.make_async_copy(a, b, sems.at[k]) for k, (a, b) in enumerate(zip(sources, held_refs))]
    for c in copies:
        c.start()
    out_ref[3 * held :] = jnp.zeros((layout.slots - 3 * held, *out_ref.shape[1:]), F32)
    for c in copies:
        c.wait()
    *fields, p, source, loc, trace, w, exp, count_ref = held_refs
    for first in range(0, held, own):
        for k, field in enumerate(fields):
            put_parts(out_ref, (), k * held + first, to_parts(field, first, own, J))
        put_parts(p_ref, (), first, to_parts(p, first, own, J))
        parts = to_parts(source.at[0], first, own, J)
        for z in range(blocks_ref.shape[0]):
            put_parts(blocks_ref, (z,), first, parts)
    shape = w.shape
    index = lax.broadcasted_iota(jnp.int32, shape, 0) * LANES + lax.broadcasted_iota(jnp.int32, shape, 1)
    layout.put(out_ref, 0, layout.place(loc[...]).astype(F32))
    layout.put(out_ref, 1, trace[...].astype(F32))
    layout.put(out_ref, 2, jnp.where(index < count_ref[0], w[...], 0.0))
    layout.put(out_ref, 3, layout.place(exp[...]).astype(F32))


def hot_rows(layout, ent_ref, rt_ref):
    parts, rows, entries = rt_ref.shape
    iota = lax.broadcasted_iota(jnp.int32, (rows, LANES), 0)
    for d in range(parts):
        row = layout.entries(ent_ref, d, 0).astype(jnp.int32) // LANES % rows
        for m in range(entries // LANES):
            at = slice(m * LANES, (m + 1) * LANES)
            rt_ref[d, :, at] = jnp.where(iota == row[m : m + 1, :], 1.0, 0.0).astype(BF16)


def prep_kernel(layout, *refs):
    *piece_refs, fld_ref, ent_ref, l_ref, rt_ref = refs
    parts, rows, entries = rt_ref.shape
    held, own = layout.held, layout.own
    inner = held // own
    far, near = lax.axis_index("fo"), lax.axis_index("fi")
    pair = len(piece_refs)
    outer = parts // pair
    for i in range(pair):
        for o in range(outer):
            d = lax.rem(far - o + outer, outer) * pair + lax.rem(near - i + pair, pair)
            for k in range(3):
                for x in range(inner):
                    at = k * held + x * own
                    fld_ref[k, d * inner + x] = piece_refs[i][o, at : at + own]
            for slot in range(layout.slots - 3 * held):
                at = slot * layout.frac_rows
                ent_ref[d, at : at + layout.frac_rows, :] = piece_refs[i][o, 3 * held + slot]
    hot_rows(layout, ent_ref, rt_ref)
    for d in range(parts):
        cell = layout.entries(ent_ref, d, 0).astype(jnp.int32)
        col, half = cell % LANES, cell // LANES // rows
        for m in range(entries // LANES):
            at = slice(m * LANES, (m + 1) * LANES)
            iota_l = lax.broadcasted_iota(jnp.int32, (LANES, LANES), 0)
            for h in range(l_ref.shape[2] // LANES):
                mine = (iota_l == col[m : m + 1, :]) & (half[m : m + 1, :] == h)
                l_ref[d, at, h * LANES : (h + 1) * LANES] = jnp.where(mine, 1.0, 0.0).T.astype(BF16)
        tis = scatter_rows(split_high_low(layout.entries(ent_ref, d, 2), 3), rt_ref, l_ref, d)
        fld_ref[3, d * inner : (d + 1) * inner] = tis.reshape(inner, *fld_ref.shape[2:])


def couple(o_ref, c_ref, ent_ref, layout, rt_ref, l_ref):
    parts = rt_ref.shape[0]
    frac_rows, own = layout.frac_rows, layout.own
    inner = layout.held // own
    rows = layout.held * frac_rows
    export_rows = layout.export_rows
    iota = lax.broadcasted_iota(jnp.int32, (SUBS, LANES), 0)
    exported = []
    for d in range(parts):
        cell = layout.entries(ent_ref, d, 3).astype(jnp.int32)
        for e in range(export_rows):
            at = jnp.broadcast_to(cell[e : e + 1, :], (SUBS, LANES))
            row, col = at // LANES - iota, at % LANES
            found = [jnp.zeros((SUBS, LANES), F32) for _ in range(2)]
            for t in range(rows // SUBS):
                slot, r = t * SUBS // frac_rows, t * SUBS % frac_rows
                got = pick_lanes(o_ref[d * inner + slot // own, slot % own, r : r + SUBS, :], col)
                found[t % 2] = jnp.where(row == t * SUBS, got, found[t % 2])
            exported.append(jnp.sum(found[0] + found[1], axis=0, keepdims=True))
    for d in range(parts):
        slot = layout.entries(ent_ref, d, 1).astype(jnp.int32)
        row, col = slot // LANES, slot % LANES
        x = jnp.zeros(slot.shape, F32)
        for t in range(parts * export_rows):
            if t // export_rows != d:
                got = pick_lanes(jnp.broadcast_to(exported[t], slot.shape), col)
                x = jnp.where(row == t, got, x)
        c = scatter_rows(split_high_low(layout.entries(ent_ref, d, 2) * x, 2), rt_ref, l_ref, d)
        c_ref[d * inner : (d + 1) * inner] = c.reshape(inner, *o_ref.shape[1:])


def fine_kernel(layout, u_ref, s_ref, fld_ref, ent_ref, l_ref, o_ref, c_ref, rt_ref):
    total = o_ref.shape[0]
    own, J = layout.own, layout.J
    group = math.gcd(total, 8)
    hot_rows(layout, ent_ref, rt_ref)
    o_ref[...] = u_ref[:, 0] if len(u_ref.shape) == 5 else u_ref[...]

    def step(_, carry):
        couple(o_ref, c_ref, ent_ref, layout, rt_ref, l_ref)

        def turn(g, carry):
            at = pl.ds(g * group, group)
            q, c = (parts_of(ref, (at,), 0, own, J) for ref in (o_ref, c_ref))
            sto, per, lea, tis = (parts_of(fld_ref, (k, at), 0, own, J) for k in range(4))
            s = parts_of(s_ref, (at, 1), 0, own, J)
            put_parts(o_ref, (at,), 0, implicit(q, s, c, sto, per, lea, tis, fine_size, SWEEPS))
            return carry

        return lax.fori_loop(0, total // group, turn, carry)

    lax.fori_loop(0, FINE_STEPS, step, 0)


def chain_kernel(layout, kind, *refs):
    if kind == 0:
        p_ref, field_ref, s_ref, u_ref = refs
    elif kind == 1:
        p_ref, field_ref, s_ref, f_ref, old_ref, u_ref, g_ref = refs
    else:
        p_ref, field_ref, s_ref, f_ref, old_ref, out_ref, u_ref = refs
    slices = s_ref.shape[0]
    held, own, J = layout.held, layout.own, layout.J
    inner = held // own
    x = lax.axis_index("x")

    def parts(ref, *index, first=0):
        return [[y[None] for y in part] for part in parts_of(ref, index, first, own, J)]

    def put(ref, index, value):
        put_parts(ref, index, 0, [[y[0] for y in part] for part in value])

    mine = (lax.axis_index("fo") * layout.pair + lax.axis_index("fi")) * inner + x
    sto, per, lea = (parts(field_ref, k, mine) for k in range(3))
    at = (lambda n: (n, 0)) if kind == 0 else (lambda n: (n,))
    start = parts(p_ref, first=x * own)
    put(u_ref, at(0), start)
    if kind == 0:
        u_ref[:, 1] = s_ref[...]

    def turn(n, u):
        g = implicit(u, parts(s_ref, n), None, sto, per, lea, None, fine_size * FINE_STEPS, COARSE_SWEEPS)
        if kind:
            f = parts(f_ref, n)
            old = parts(old_ref, n + 1, 0) if len(old_ref.shape) == 5 else parts(old_ref, n)
            if kind == 1:
                put(g_ref, (n,), g)
            g = [[g[k][j] + (f[k][j] - old[k][j]) for j in range(J)] for k in range(own)]
        put(u_ref, at(n + 1), g)
        return g

    lax.fori_loop(0, slices - 1, turn, start)
    if kind == 1:
        g_ref[slices - 1] = jnp.zeros(g_ref.shape[1:], F32)
    if kind == 2:
        z = lax.axis_index("z")
        for k in range(inner):
            n = z * inner + lax.rem(x + k, inner)
            from_parts(out_ref, (k,), parts_of(u_ref, (n,), 0, own, J))


def gather_from(axis, a):
    n = lax.axis_size(axis)
    return [a] + [lax.ppermute(a, axis, [(i, (i + k) % n) for i in range(n)]) for k in range(1, n)]


def body(sizes, pressure0, storage, perm_base, leakoff, sources, export_cells, inter_local, trace_source, inter_trans, inter_count):
    groups, inner, outer, pair = sizes
    fracs = outer * pair
    slices = groups * inner
    held, frac_rows, _ = pressure0.shape
    own = held // inner
    plane = ("fo", "fi", "x")
    layout = Layout(held, own, pair, frac_rows, inter_local.size, export_cells.size)
    block = (own, frac_rows, LANES)
    plain = shape_of(slices, *block)

    lists = [a.reshape(-1, LANES) for a in (inter_local, trace_source, inter_trans, export_cells)]
    arrays = (storage, perm_base, leakoff, pressure0, sources, *lists, inter_count)
    packed, blocks, start = call(
        functools.partial(pack_kernel, layout),
        "pack",
        arrays,
        (shape_of(layout.slots, frac_rows, LANES), shape_of(groups, *pressure0.shape), shape_of(*pressure0.shape)),
        [pltpu.VMEM(a.shape, a.dtype) for a in arrays[:-1]]
        + [pltpu.SMEM(inter_count.shape, jnp.int32), pltpu.SemaphoreType.DMA((len(arrays),))],
        [HBM] * len(arrays),
        56 * 2**20,
    )
    far = gather_from("fo", packed[None])
    own_sources = lax.all_to_all(blocks.reshape(plain.shape), ("z", "x"), 0, 0, tiled=True)
    pieces = gather_from("fi", jnp.concatenate(far, axis=0))
    hot = pltpu.VMEM((fracs, held * frac_rows // 2, inter_local.size), BF16)
    fld, ent, l = call(
        functools.partial(prep_kernel, layout),
        "prep",
        pieces,
        (
            shape_of(4, slices, *block),
            shape_of(fracs, (layout.slots - 3 * held) * frac_rows, LANES),
            shape_of(fracs, inter_local.size, 2 * LANES, dtype=BF16),
        ),
        [hot],
    )
    own_sources, fld, ent, l = lax.optimization_barrier((own_sources, fld, ent, l))

    base = (start, fld, own_sources)
    (u0,) = call(functools.partial(chain_kernel, layout, 0), "chain0", base, (shape_of(slices, 2, *block),))
    b0 = lax.all_to_all(u0, plane, 0, 0, tiled=True)
    u, old = b0, u0
    for iteration in range(ITERS):
        (ends,) = call(
            functools.partial(fine_kernel, layout),
            "fine",
            (u, b0, fld, ent, l),
            (plain,),
            [pltpu.VMEM(plain.shape, F32), hot],
        )
        ends = lax.all_to_all(ends, plane, 0, 0, tiled=True)
        if iteration < ITERS - 1:
            states, old = call(functools.partial(chain_kernel, layout, 1), "chain1", (*base, ends, old), (plain, plain))
            u = lax.all_to_all(states, plane, 0, 0, tiled=True)
    (mine,) = call(
        functools.partial(chain_kernel, layout, 2),
        "chain2",
        (*base, ends, old),
        (shape_of(inner, *block),),
        [pltpu.VMEM(plain.shape, F32)],
    )
    x = lax.axis_index("x")
    got = [mine[0]] + [
        lax.ppermute(mine[k], "x", [(i, (i + k) % inner) for i in range(inner)]) for k in range(1, inner)
    ]
    return jnp.stack([lax.select_n((x - i) % inner, *got) if inner > 2 else jnp.where(x == i, got[0], got[-1]) for i in range(inner)]).reshape(1, held, frac_rows, LANES)


def solution(mesh):
    slices, fracs = mesh.shape["tm"], mesh.shape["frac"]
    inner = slices // fracs
    pair = math.gcd(fracs, 2)
    sizes = (slices // inner, inner, fracs // pair, pair)
    mesh = Mesh(mesh.devices.reshape(sizes), ("z", "x", "fo", "fi"))
    frac = P(("fo", "fi"))
    both = P(("z", "x"), ("fo", "fi"))
    return jax.shard_map(
        functools.partial(body, sizes),
        mesh=mesh,
        in_specs=(frac,) * 4 + (both,) + (frac,) * 5,
        out_specs=both,
        check_vma=False,
    )
```

```python
import functools
import math

import jax
import jax.numpy as jnp
from jax import lax
from jax.experimental import pallas as pl
from jax.experimental.pallas import tpu as pltpu
from jax.sharding import Mesh, PartitionSpec as P

FINE_STEPS = 4
SWEEPS = 8
COARSE_SWEEPS = 2
ITERS = 2

stress_factor = 0.15
fine_size = 0.25

LANES = 128
SUBS = 8
F32 = jnp.float32
BF16 = jnp.bfloat16
VMEM = pl.BlockSpec(memory_space=pltpu.VMEM)
HBM = pl.BlockSpec(memory_space=pltpu.HBM)


def shape_of(*dims, dtype=F32):
    return jax.ShapeDtypeStruct(dims, dtype)


def call(kernel, name, args, outs, scratch=(), specs=None, room=4 * 2**20):
    size = sum(math.prod(a.shape) * a.dtype.itemsize for a in (*args, *outs))
    return pl.pallas_call(
        kernel,
        out_shape=outs,
        in_specs=specs or [VMEM] * len(args),
        out_specs=(VMEM,) * len(outs),
        scratch_shapes=scratch,
        compiler_params=pltpu.CompilerParams(vmem_limit_bytes=room + size),
        name=name,
    )(*args)


def lane_roll(x, s):
    return pltpu.roll(x, s % LANES, axis=2)


def sub_roll(x, s):
    return pltpu.roll(x, s % SUBS, axis=1)


def coefficients(q, sto, per, lea, tis, step_size):
    M, J = len(q), len(q[0])
    shape = q[0][0].shape
    row = lax.broadcasted_iota(jnp.int32, shape, 1)
    col = lax.broadcasted_iota(jnp.int32, shape, 2) % (LANES // M)

    def each(f):
        return [[f(k, j) for j in range(J)] for k in range(M)]

    half = each(lambda k, j: (0.5 * per[k][j]) * jnp.exp(stress_factor * q[k][j]))
    down, up, right, left = neighbours(half, rolled(half))
    row_next = each(lambda k, j: half[k][j] + down[k][j])
    row_prev = each(lambda k, j: half[k][j] + up[k][j] if j == 0 else row_next[k][j - 1])
    col_next = each(lambda k, j: half[k][j] + right[k][j])
    col_prev = each(lambda k, j: half[k][j] + left[k][j] if k == 0 else col_next[k - 1][j])
    for k in range(M):
        row_next[k][J - 1] = jnp.where(row == SUBS - 1, 0.0, row_next[k][J - 1])
        row_prev[k][0] = jnp.where(row == 0, 0.0, row_prev[k][0])
    for j in range(J):
        col_next[M - 1][j] = jnp.where(col == LANES // M - 1, 0.0, col_next[M - 1][j])
        col_prev[0][j] = jnp.where(col == 0, 0.0, col_prev[0][j])

    def inverse(k, j):
        total = sto[k][j] * (1.0 / step_size) + lea[k][j]
        if tis is not None:
            total = total + tis[k][j]
        return 1.0 / ((total + (row_next[k][j] + row_prev[k][j])) + (col_next[k][j] + col_prev[k][j]))

    inv = each(inverse)
    return [inv] + [each(lambda k, j: t[k][j] * inv[k][j]) for t in (row_next, row_prev, col_next, col_prev)]


def rolled(v):
    return (
        [sub_roll(part[0], -1) for part in v],
        [sub_roll(part[-1], 1) for part in v],
        [lane_roll(x, -1) for x in v[0]],
        [lane_roll(x, 1) for x in v[-1]],
    )


def neighbours(v, edges):
    after, before, right, left = edges
    return (
        [part[1:] + [after[k]] for k, part in enumerate(v)],
        [[before[k]] + part[:-1] for k, part in enumerate(v)],
        v[1:] + [right],
        [left] + v[:-1],
    )


def implicit(q, sto, per, lea, tis, sources, step_size, sweeps):
    M, J = len(q[0]), len(q[0][0])
    grid = [(k, j) for k in range(M) for j in range(J)]
    blocks = range(len(q))
    known, edges, rhs = [], [], []
    for b in blocks:
        s = sources(b)
        known.append(coefficients(q[b], sto[b], per[b], lea[b], None if tis is None else tis[b], step_size))
        edges.append(rolled(q[b]))
        inv = known[b][0]
        rhs.append([[None] * J for _ in range(M)])
        for k, j in grid:
            rhs[b][k][j] = (sto[b][k][j] * (1.0 / step_size) * q[b][k][j] + s[k][j]) * inv[k][j]
    v = list(q)
    for sweep in range(sweeps):
        for b in blocks:
            _, a_rn, a_rp, a_cn, a_cp = known[b]
            down, up, right, left = neighbours(v[b], edges[b])
            new = [[None] * J for _ in range(M)]
            for k, j in grid:
                new[k][j] = (rhs[b][k][j] + a_rn[k][j] * down[k][j] + a_rp[k][j] * up[k][j]) + (
                    a_cn[k][j] * right[k][j] + a_cp[k][j] * left[k][j]
                )
            v[b] = new
            if sweep < sweeps - 1:
                edges[b] = rolled(new)
    return v


def parts_of(ref, index, first, M, J):
    return [[ref[(*index, first + k, pl.ds(j * SUBS, SUBS), slice(None))] for j in range(J)] for k in range(M)]


def put_parts(ref, index, first, parts):
    for k, part in enumerate(parts):
        for j, x in enumerate(part):
            ref[(*index, first + k, pl.ds(j * SUBS, SUBS), slice(None))] = x


def pick_lanes(x, index):
    return jnp.take_along_axis(x, index, axis=1, mode="promise_in_bounds")


def to_parts(ref, first, M, J):
    lane = lax.broadcasted_iota(jnp.int32, (SUBS, LANES), 1)
    width = LANES // M
    out = [[None] * J for _ in range(M)]
    for j in range(J):
        rows = [ref[first + f, pl.ds(j, SUBS, stride=J), :] for f in range(M)]
        for k in range(M):
            x = pick_lanes(rows[0], lane % width * M + k)
            for f in range(1, M):
                x = jnp.where(lane // width == f, pick_lanes(rows[f], lane % width * M + k), x)
            out[k][j] = x
    return out


def from_parts(ref, index, parts):
    lane = lax.broadcasted_iota(jnp.int32, (SUBS, LANES), 1)
    M, J = len(parts), len(parts[0])
    width = LANES // M
    for j in range(J):
        for f in range(M):
            x = pick_lanes(parts[0][j], lane // M + f * width)
            for k in range(1, M):
                x = jnp.where(lane % M == k, pick_lanes(parts[k][j], lane // M + f * width), x)
            ref[(*index, f, pl.ds(j, SUBS, stride=J), slice(None))] = x


def split_high_low(x, pieces):
    out = []
    for _ in range(pieces):
        part = x.astype(BF16).astype(F32)
        out.append(part)
        x = x - part
    return out


def scatter_rows(values, rt_ref, l_ref, d):
    rows, entries = rt_ref.shape[1:]
    pieces = []
    for value in values:
        cols = []
        for m in range(entries // LANES):
            row = jnp.broadcast_to(value[m : m + 1, :], (2 * SUBS, LANES)).astype(BF16)
            hot = rt_ref[d, :, m * LANES : (m + 1) * LANES].reshape(-1, 2 * SUBS, LANES)
            cols.append((hot * row[None]).reshape(rows, LANES))
        pieces.append(jnp.concatenate(cols, axis=1))
    both = jnp.dot(jnp.concatenate(pieces, axis=0), l_ref[d], preferred_element_type=F32)
    out = both[:rows]
    for i in range(1, len(values)):
        out = out + both[i * rows : (i + 1) * rows]
    return jnp.concatenate([out[:, h * LANES : (h + 1) * LANES] for h in range(out.shape[1] // LANES)], axis=0)


class Layout:
    def __init__(self, held, own, pair, frac_rows, entries, exports):
        self.held, self.own, self.pair, self.frac_rows = held, own, pair, frac_rows
        self.J = frac_rows // SUBS
        self.entry_rows = entries // LANES
        self.export_rows = exports // LANES
        padded = -(-self.export_rows // SUBS) * SUBS
        self.sizes = [self.entry_rows] * 3 + [self.export_rows]
        self.slots = 3 * held + -(-(3 * self.entry_rows + padded) // frac_rows)

    def place(self, cell):
        own, J = self.own, self.J
        f, row, col = cell // (self.frac_rows * LANES), cell // LANES % self.frac_rows, cell % LANES
        part = (f // own * own + col % own) * J + row % J
        return (part * SUBS + row // J) * LANES + f % own * (LANES // own) + col // own

    def entries(self, ref, d, kind):
        start = kind * self.entry_rows
        return ref[d, start : start + self.sizes[kind], :]

    def put(self, ref, kind, value):
        at, left, start = 0, self.sizes[kind], kind * self.entry_rows
        while left:
            n = min(left, SUBS)
            slot, r = 3 * self.held + start // self.frac_rows, start % self.frac_rows
            ref[slot, r : r + n, :] = value[at : at + n]
            at, start, left = at + n, start + n, left - n


def pack_kernel(layout, *refs):
    sources = refs[:10]
    out_ref, blocks_ref, p_ref = refs[10:13]
    held_refs, sems = refs[13:23], refs[23]
    held, own, J = layout.held, layout.own, layout.J
    copies = [pltpu.make_async_copy(a, b, sems.at[k]) for k, (a, b) in enumerate(zip(sources, held_refs))]
    for c in copies:
        c.start()
    out_ref[3 * held :] = jnp.zeros((layout.slots - 3 * held, *out_ref.shape[1:]), F32)
    for c in copies:
        c.wait()
    *fields, p, source, loc, trace, w, exp, count_ref = held_refs
    for first in range(0, held, own):
        for k, field in enumerate(fields):
            put_parts(out_ref, (), k * held + first, to_parts(field, first, own, J))
        put_parts(p_ref, (), first, to_parts(p, first, own, J))
        parts = to_parts(source.at[0], first, own, J)
        for z in range(blocks_ref.shape[0]):
            put_parts(blocks_ref, (z,), first, parts)
    shape = w.shape
    index = lax.broadcasted_iota(jnp.int32, shape, 0) * LANES + lax.broadcasted_iota(jnp.int32, shape, 1)
    layout.put(out_ref, 0, layout.place(loc[...]).astype(F32))
    layout.put(out_ref, 1, trace[...].astype(F32))
    layout.put(out_ref, 2, jnp.where(index < count_ref[0], w[...], 0.0))
    layout.put(out_ref, 3, layout.place(exp[...]).astype(F32))


def hot_rows(layout, ent_ref, rt_ref):
    parts, rows, entries = rt_ref.shape
    iota = lax.broadcasted_iota(jnp.int32, (rows, LANES), 0)
    for d in range(parts):
        row = layout.entries(ent_ref, d, 0).astype(jnp.int32) // LANES % rows
        for m in range(entries // LANES):
            at = slice(m * LANES, (m + 1) * LANES)
            rt_ref[d, :, at] = jnp.where(iota == row[m : m + 1, :], 1.0, 0.0).astype(BF16)


def prep_kernel(layout, *refs):
    *piece_refs, fld_ref, ent_ref, l_ref, rt_ref = refs
    parts, rows, entries = rt_ref.shape
    held, own = layout.held, layout.own
    inner = held // own
    far, near = lax.axis_index("fo"), lax.axis_index("fi")
    pair = len(piece_refs)
    outer = parts // pair
    for i in range(pair):
        for o in range(outer):
            d = lax.rem(far - o + outer, outer) * pair + lax.rem(near - i + pair, pair)
            for k in range(3):
                for x in range(inner):
                    at = k * held + x * own
                    fld_ref[k, d * inner + x] = piece_refs[i][o, at : at + own]
            for slot in range(layout.slots - 3 * held):
                at = slot * layout.frac_rows
                ent_ref[d, at : at + layout.frac_rows, :] = piece_refs[i][o, 3 * held + slot]
    hot_rows(layout, ent_ref, rt_ref)
    for d in range(parts):
        cell = layout.entries(ent_ref, d, 0).astype(jnp.int32)
        col, half = cell % LANES, cell // LANES // rows
        for m in range(entries // LANES):
            at = slice(m * LANES, (m + 1) * LANES)
            iota_l = lax.broadcasted_iota(jnp.int32, (LANES, LANES), 0)
            for h in range(l_ref.shape[2] // LANES):
                mine = (iota_l == col[m : m + 1, :]) & (half[m : m + 1, :] == h)
                l_ref[d, at, h * LANES : (h + 1) * LANES] = jnp.where(mine, 1.0, 0.0).T.astype(BF16)
        tis = scatter_rows(split_high_low(layout.entries(ent_ref, d, 2), 3), rt_ref, l_ref, d)
        fld_ref[3, d * inner : (d + 1) * inner] = tis.reshape(inner, *fld_ref.shape[2:])


def arriving(o_ref, ent_ref, layout, parts):
    frac_rows, own = layout.frac_rows, layout.own
    inner = layout.held // own
    rows = layout.held * frac_rows
    export_rows = layout.export_rows
    iota = lax.broadcasted_iota(jnp.int32, (SUBS, LANES), 0)
    exported = []
    for d in range(parts):
        cell = layout.entries(ent_ref, d, 3).astype(jnp.int32)
        for e in range(export_rows):
            at = jnp.broadcast_to(cell[e : e + 1, :], (SUBS, LANES))
            row, col = at // LANES - iota, at % LANES
            found = [jnp.zeros((SUBS, LANES), F32) for _ in range(2)]
            for t in range(rows // SUBS):
                slot, r = t * SUBS // frac_rows, t * SUBS % frac_rows
                got = pick_lanes(o_ref[d * inner + slot // own, slot % own, r : r + SUBS, :], col)
                found[t % 2] = jnp.where(row == t * SUBS, got, found[t % 2])
            exported.append(jnp.sum(found[0] + found[1], axis=0, keepdims=True))
    out = []
    for d in range(parts):
        slot = layout.entries(ent_ref, d, 1).astype(jnp.int32)
        row, col = slot // LANES, slot % LANES
        x = jnp.zeros(slot.shape, F32)
        for t in range(parts * export_rows):
            if t // export_rows != d:
                got = pick_lanes(jnp.broadcast_to(exported[t], slot.shape), col)
                x = jnp.where(row == t, got, x)
        out.append(layout.entries(ent_ref, d, 2) * x)
    return out


def fine_kernel(layout, u_ref, s_ref, fld_ref, ent_ref, l_ref, o_ref, c_ref, rt_ref):
    total = o_ref.shape[0]
    own, J = layout.own, layout.J
    group = math.gcd(total, 8)
    hot_rows(layout, ent_ref, rt_ref)
    o_ref[...] = u_ref[:, 0] if len(u_ref.shape) == 5 else u_ref[...]

    fracs, inner = rt_ref.shape[0], layout.held // own

    def couple(d, values):
        c = scatter_rows(split_high_low(values, 2), rt_ref, l_ref, d)
        c_ref[d * inner : (d + 1) * inner] = c.reshape(inner, *c_ref.shape[1:])

    def one_step(first):
        def blocks(ref, *index):
            return [parts_of(ref, (*index, pl.ds(first + b, 1)), 0, own, J) for b in range(group)]

        def sources(b):
            c = parts_of(c_ref, (pl.ds(first + b, 1),), 0, own, J)
            s = parts_of(s_ref, (pl.ds(first + b, 1), 1), 0, own, J)
            return [[s[k][j] + c[k][j] for j in range(J)] for k in range(own)]

        sto, per, lea, tis = (blocks(fld_ref, k) for k in range(4))
        out = implicit(blocks(o_ref), sto, per, lea, tis, sources, fine_size, SWEEPS)
        for b in range(group):
            put_parts(o_ref, (pl.ds(first + b, 1),), 0, out[b])

    def step(_, carry):
        values = arriving(o_ref, ent_ref, layout, fracs)
        for d in range(fracs):
            couple(d, values[d])

        def turn(g, carry):
            one_step(g * group)
            return carry

        return turn(0, carry) if total == group else lax.fori_loop(0, total // group, turn, carry)

    lax.fori_loop(0, FINE_STEPS, step, 0)


def chain_kernel(layout, kind, done, *refs):
    if kind == 0:
        p_ref, field_ref, s_ref, u_ref = refs
    elif kind == 1:
        p_ref, field_ref, s_ref, f_ref, old_ref, u_ref, g_ref = refs
    else:
        p_ref, field_ref, s_ref, f_ref, old_ref, out_ref, u_ref = refs
    slices = s_ref.shape[0]
    held, own, J = layout.held, layout.own, layout.J
    inner = held // own
    x = lax.axis_index("x")

    def parts(ref, *index, first=0):
        return [[y[None] for y in part] for part in parts_of(ref, index, first, own, J)]

    def put(ref, index, value):
        put_parts(ref, index, 0, [[y[0] for y in part] for part in value])

    mine = (lax.axis_index("fo") * layout.pair + lax.axis_index("fi")) * inner + x
    sto, per, lea = (parts(field_ref, k, mine) for k in range(3))
    at = (lambda n: (n, 0)) if kind == 0 else (lambda n: (n,))
    start = parts(p_ref, first=x * own)
    put(u_ref, at(0), start)
    if kind == 0:
        u_ref[:, 1] = s_ref[...]

    def turn(n, u):
        sources = lambda b: parts(s_ref, n)
        (g,) = implicit([u], [sto], [per], [lea], None, sources, fine_size * FINE_STEPS, COARSE_SWEEPS)
        if kind:
            f = parts(f_ref, n)
            old = parts(old_ref, n + 1, 0) if len(old_ref.shape) == 5 else parts(old_ref, n)
            if kind == 1:
                put(g_ref, (n,), g)
            g = [[g[k][j] + (f[k][j] - old[k][j]) for j in range(J)] for k in range(own)]
        put(u_ref, at(n + 1), g)
        return g

    for n in range(done):
        start = parts(f_ref, n)
        put(u_ref, at(n + 1), start)
        if kind == 1:
            g_ref[n] = jnp.zeros(g_ref.shape[1:], F32)
    lax.fori_loop(done, slices - 1, turn, start)
    if kind == 1:
        g_ref[slices - 1] = jnp.zeros(g_ref.shape[1:], F32)
    if kind == 2:
        z = lax.axis_index("z")
        for k in range(inner):
            n = z * inner + lax.rem(x + k, inner)
            from_parts(out_ref, (k,), parts_of(u_ref, (n,), 0, own, J))


def gather_from(axis, a):
    n = lax.axis_size(axis)
    return [a] + [lax.ppermute(a, axis, [(i, (i + k) % n) for i in range(n)]) for k in range(1, n)]


def body(sizes, pressure0, storage, perm_base, leakoff, sources, export_cells, inter_local, trace_source, inter_trans, inter_count):
    groups, inner, outer, pair = sizes
    fracs = outer * pair
    slices = groups * inner
    held, frac_rows, _ = pressure0.shape
    own = held // inner
    plane = ("fo", "fi", "x")
    layout = Layout(held, own, pair, frac_rows, inter_local.size, export_cells.size)
    block = (own, frac_rows, LANES)
    plain = shape_of(slices, *block)

    lists = [a.reshape(-1, LANES) for a in (inter_local, trace_source, inter_trans, export_cells)]
    arrays = (storage, perm_base, leakoff, pressure0, sources, *lists, inter_count)
    packed, blocks, start = call(
        functools.partial(pack_kernel, layout),
        "pack",
        arrays,
        (shape_of(layout.slots, frac_rows, LANES), shape_of(groups, *pressure0.shape), shape_of(*pressure0.shape)),
        [pltpu.VMEM(a.shape, a.dtype) for a in arrays[:-1]]
        + [pltpu.SMEM(inter_count.shape, jnp.int32), pltpu.SemaphoreType.DMA((len(arrays),))],
        [HBM] * len(arrays),
        56 * 2**20,
    )
    far = gather_from("fo", packed[None])
    own_sources = lax.all_to_all(blocks.reshape(plain.shape), ("z", "x"), 0, 0, tiled=True)
    pieces = gather_from("fi", jnp.concatenate(far, axis=0))
    hot = pltpu.VMEM((fracs, held * frac_rows // 2, inter_local.size), BF16)
    fld, ent, l = call(
        functools.partial(prep_kernel, layout),
        "prep",
        pieces,
        (
            shape_of(4, slices, *block),
            shape_of(fracs, (layout.slots - 3 * held) * frac_rows, LANES),
            shape_of(fracs, inter_local.size, 2 * LANES, dtype=BF16),
        ),
        [hot],
    )
    own_sources, fld, ent, l = lax.optimization_barrier((own_sources, fld, ent, l))

    base = (start, fld, own_sources)
    (u0,) = call(functools.partial(chain_kernel, layout, 0, 0), "chain0", base, (shape_of(slices, 2, *block),))
    b0 = lax.all_to_all(u0, plane, 0, 0, tiled=True)
    u, old = b0, u0
    for iteration in range(ITERS):
        (ends,) = call(
            functools.partial(fine_kernel, layout),
            "fine",
            (u, b0, fld, ent, l),
            (plain,),
            [pltpu.VMEM(plain.shape, F32), hot],
        )
        ends = lax.all_to_all(ends, plane, 0, 0, tiled=True)
        if iteration < ITERS - 1:
            states, old = call(functools.partial(chain_kernel, layout, 1, iteration + 1), "chain1", (*base, ends, old), (plain, plain))
            u = lax.all_to_all(states, plane, 0, 0, tiled=True)
    (mine,) = call(
        functools.partial(chain_kernel, layout, 2, ITERS),
        "chain2",
        (*base, ends, old),
        (shape_of(inner, *block),),
        [pltpu.VMEM(plain.shape, F32)],
    )
    x = lax.axis_index("x")
    got = [mine[0]] + [
        lax.ppermute(mine[k], "x", [(i, (i + k) % inner) for i in range(inner)]) for k in range(1, inner)
    ]
    return jnp.stack([lax.select_n((x - i) % inner, *got) if inner > 2 else jnp.where(x == i, got[0], got[-1]) for i in range(inner)]).reshape(1, held, frac_rows, LANES)


def solution(mesh):
    slices, fracs = mesh.shape["tm"], mesh.shape["frac"]
    inner = slices // fracs
    pair = math.gcd(fracs, 2)
    sizes = (slices // inner, inner, fracs // pair, pair)
    mesh = Mesh(mesh.devices.reshape(sizes), ("z", "x", "fo", "fi"))
    frac = P(("fo", "fi"))
    both = P(("z", "x"), ("fo", "fi"))
    return jax.shard_map(
        functools.partial(body, sizes),
        mesh=mesh,
        in_specs=(frac,) * 4 + (both,) + (frac,) * 5,
        out_specs=both,
        check_vma=False,
    )
```

```python
import functools
import math

import jax
import jax.numpy as jnp
from jax import lax
from jax.experimental import pallas as pl
from jax.experimental.pallas import tpu as pltpu
from jax.sharding import Mesh, PartitionSpec as P

FINE_STEPS = 4
SWEEPS = 8
COARSE_SWEEPS = 2
ITERS = 2

stress_factor = 0.15
fine_size = 0.25

LANES = 128
SUBS = 8
F32 = jnp.float32
BF16 = jnp.bfloat16
VMEM = pl.BlockSpec(memory_space=pltpu.VMEM)
HBM = pl.BlockSpec(memory_space=pltpu.HBM)


def shape_of(*dims, dtype=F32):
    return jax.ShapeDtypeStruct(dims, dtype)


def call(kernel, name, args, outs, scratch=(), specs=None, room=4 * 2**20):
    size = sum(math.prod(a.shape) * a.dtype.itemsize for a in (*args, *outs))
    return pl.pallas_call(
        kernel,
        out_shape=outs,
        in_specs=specs or [VMEM] * len(args),
        out_specs=(VMEM,) * len(outs),
        scratch_shapes=scratch,
        compiler_params=pltpu.CompilerParams(vmem_limit_bytes=room + size),
        name=name,
    )(*args)


def lane_roll(x, s):
    return pltpu.roll(x, s % LANES, axis=2)


def sub_roll(x, s):
    return pltpu.roll(x, s % SUBS, axis=1)


def coefficients(q, sto, per, lea, tis, step_size):
    M, J = len(q), len(q[0])
    shape = q[0][0].shape
    row = lax.broadcasted_iota(jnp.int32, shape, 1)
    col = lax.broadcasted_iota(jnp.int32, shape, 2) % (LANES // M)

    def each(f):
        return [[f(k, j) for j in range(J)] for k in range(M)]

    half = each(lambda k, j: (0.5 * per[k][j]) * jnp.exp(stress_factor * q[k][j]))
    down, up, right, left = neighbours(half, rolled(half))
    row_next = each(lambda k, j: half[k][j] + down[k][j])
    row_prev = each(lambda k, j: half[k][j] + up[k][j] if j == 0 else row_next[k][j - 1])
    col_next = each(lambda k, j: half[k][j] + right[k][j])
    col_prev = each(lambda k, j: half[k][j] + left[k][j] if k == 0 else col_next[k - 1][j])
    for k in range(M):
        row_next[k][J - 1] = jnp.where(row == SUBS - 1, 0.0, row_next[k][J - 1])
        row_prev[k][0] = jnp.where(row == 0, 0.0, row_prev[k][0])
    for j in range(J):
        col_next[M - 1][j] = jnp.where(col == LANES // M - 1, 0.0, col_next[M - 1][j])
        col_prev[0][j] = jnp.where(col == 0, 0.0, col_prev[0][j])

    def inverse(k, j):
        total = sto[k][j] * (1.0 / step_size) + lea[k][j]
        if tis is not None:
            total = total + tis[k][j]
        return 1.0 / ((total + (row_next[k][j] + row_prev[k][j])) + (col_next[k][j] + col_prev[k][j]))

    inv = each(inverse)
    return [inv] + [each(lambda k, j: t[k][j] * inv[k][j]) for t in (row_next, row_prev, col_next, col_prev)]


def rolled(v):
    return (
        [sub_roll(part[0], -1) for part in v],
        [sub_roll(part[-1], 1) for part in v],
        [lane_roll(x, -1) for x in v[0]],
        [lane_roll(x, 1) for x in v[-1]],
    )


def neighbours(v, edges):
    after, before, right, left = edges
    return (
        [part[1:] + [after[k]] for k, part in enumerate(v)],
        [[before[k]] + part[:-1] for k, part in enumerate(v)],
        v[1:] + [right],
        [left] + v[:-1],
    )


def implicit(q, sto, per, lea, tis, sources, step_size, sweeps):
    M, J = len(q[0]), len(q[0][0])
    grid = [(k, j) for k in range(M) for j in range(J)]
    blocks = range(len(q))
    known, edges, rhs = [], [], []
    for b in blocks:
        s = sources(b)
        known.append(coefficients(q[b], sto[b], per[b], lea[b], None if tis is None else tis[b], step_size))
        edges.append(rolled(q[b]))
        inv = known[b][0]
        rhs.append([[None] * J for _ in range(M)])
        for k, j in grid:
            rhs[b][k][j] = (sto[b][k][j] * (1.0 / step_size) * q[b][k][j] + s[k][j]) * inv[k][j]
    v = list(q)
    for sweep in range(sweeps):
        for b in blocks:
            _, a_rn, a_rp, a_cn, a_cp = known[b]
            down, up, right, left = neighbours(v[b], edges[b])
            new = [[None] * J for _ in range(M)]
            for k, j in grid:
                new[k][j] = (rhs[b][k][j] + a_rn[k][j] * down[k][j] + a_rp[k][j] * up[k][j]) + (
                    a_cn[k][j] * right[k][j] + a_cp[k][j] * left[k][j]
                )
            v[b] = new
            if sweep < sweeps - 1:
                edges[b] = rolled(new)
    return v


def parts_of(ref, index, first, M, J):
    return [[ref[(*index, first + k, pl.ds(j * SUBS, SUBS), slice(None))] for j in range(J)] for k in range(M)]


def put_parts(ref, index, first, parts):
    for k, part in enumerate(parts):
        for j, x in enumerate(part):
            ref[(*index, first + k, pl.ds(j * SUBS, SUBS), slice(None))] = x


def pick_lanes(x, index):
    return jnp.take_along_axis(x, index, axis=1, mode="promise_in_bounds")


def to_parts(ref, first, M, J):
    lane = lax.broadcasted_iota(jnp.int32, (SUBS, LANES), 1)
    width = LANES // M
    out = [[None] * J for _ in range(M)]
    for j in range(J):
        rows = [ref[first + f, pl.ds(j, SUBS, stride=J), :] for f in range(M)]
        for k in range(M):
            x = pick_lanes(rows[0], lane % width * M + k)
            for f in range(1, M):
                x = jnp.where(lane // width == f, pick_lanes(rows[f], lane % width * M + k), x)
            out[k][j] = x
    return out


def from_parts(ref, index, parts):
    lane = lax.broadcasted_iota(jnp.int32, (SUBS, LANES), 1)
    M, J = len(parts), len(parts[0])
    width = LANES // M
    for j in range(J):
        for f in range(M):
            x = pick_lanes(parts[0][j], lane // M + f * width)
            for k in range(1, M):
                x = jnp.where(lane % M == k, pick_lanes(parts[k][j], lane // M + f * width), x)
            ref[(*index, f, pl.ds(j, SUBS, stride=J), slice(None))] = x


def split_high_low(x, pieces):
    out = []
    for _ in range(pieces):
        part = x.astype(BF16).astype(F32)
        out.append(part)
        x = x - part
    return out


def scatter_rows(values, rt_ref, l_ref, d):
    rows, entries = rt_ref.shape[1:]
    pieces = []
    for value in values:
        cols = []
        for m in range(entries // LANES):
            row = jnp.broadcast_to(value[m : m + 1, :], (2 * SUBS, LANES)).astype(BF16)
            hot = rt_ref[d, :, m * LANES : (m + 1) * LANES].reshape(-1, 2 * SUBS, LANES)
            cols.append((hot * row[None]).reshape(rows, LANES))
        pieces.append(jnp.concatenate(cols, axis=1))
    both = jnp.dot(jnp.concatenate(pieces, axis=0), l_ref[d], preferred_element_type=F32)
    out = both[:rows]
    for i in range(1, len(values)):
        out = out + both[i * rows : (i + 1) * rows]
    return jnp.concatenate([out[:, h * LANES : (h + 1) * LANES] for h in range(out.shape[1] // LANES)], axis=0)


class Layout:
    def __init__(self, held, own, pair, frac_rows, entries, exports):
        self.held, self.own, self.pair, self.frac_rows = held, own, pair, frac_rows
        self.J = frac_rows // SUBS
        self.entry_rows = entries // LANES
        self.export_rows = exports // LANES
        padded = -(-self.export_rows // SUBS) * SUBS
        self.sizes = [self.entry_rows] * 3 + [self.export_rows]
        self.slots = 3 * held + -(-(3 * self.entry_rows + padded) // frac_rows)

    def place(self, cell):
        own, J = self.own, self.J
        f, row, col = cell // (self.frac_rows * LANES), cell // LANES % self.frac_rows, cell % LANES
        part = (f // own * own + col % own) * J + row % J
        return (part * SUBS + row // J) * LANES + f % own * (LANES // own) + col // own

    def entries(self, ref, d, kind):
        start = kind * self.entry_rows
        return ref[d, start : start + self.sizes[kind], :]

    def put(self, ref, kind, value):
        at, left, start = 0, self.sizes[kind], kind * self.entry_rows
        while left:
            n = min(left, SUBS)
            slot, r = 3 * self.held + start // self.frac_rows, start % self.frac_rows
            ref[slot, r : r + n, :] = value[at : at + n]
            at, start, left = at + n, start + n, left - n


def pack_kernel(layout, *refs):
    sources = refs[:10]
    out_ref, blocks_ref, p_ref = refs[10:13]
    held_refs, sems = refs[13:23], refs[23]
    held, own, J = layout.held, layout.own, layout.J
    copies = [pltpu.make_async_copy(a, b, sems.at[k]) for k, (a, b) in enumerate(zip(sources, held_refs))]
    for c in copies:
        c.start()
    out_ref[3 * held :] = jnp.zeros((layout.slots - 3 * held, *out_ref.shape[1:]), F32)
    for c in copies:
        c.wait()
    *fields, p, source, loc, trace, w, exp, count_ref = held_refs
    for first in range(0, held, own):
        for k, field in enumerate(fields):
            put_parts(out_ref, (), k * held + first, to_parts(field, first, own, J))
        put_parts(p_ref, (), first, to_parts(p, first, own, J))
        parts = to_parts(source.at[0], first, own, J)
        for z in range(blocks_ref.shape[1]):
            put_parts(blocks_ref, (first // own, z), 0, parts)
    shape = w.shape
    index = lax.broadcasted_iota(jnp.int32, shape, 0) * LANES + lax.broadcasted_iota(jnp.int32, shape, 1)
    layout.put(out_ref, 0, layout.place(loc[...]).astype(F32))
    layout.put(out_ref, 1, trace[...].astype(F32))
    layout.put(out_ref, 2, jnp.where(index < count_ref[0], w[...], 0.0))
    layout.put(out_ref, 3, layout.place(exp[...]).astype(F32))


def hot_rows(layout, ent_ref, rt_ref):
    parts, rows, entries = rt_ref.shape
    iota = lax.broadcasted_iota(jnp.int32, (rows, LANES), 0)
    for d in range(parts):
        row = layout.entries(ent_ref, d, 0).astype(jnp.int32) // LANES % rows
        for m in range(entries // LANES):
            at = slice(m * LANES, (m + 1) * LANES)
            rt_ref[d, :, at] = jnp.where(iota == row[m : m + 1, :], 1.0, 0.0).astype(BF16)


def prep_kernel(layout, *refs):
    *piece_refs, fld_ref, ent_ref, l_ref, rt_ref = refs
    parts, rows, entries = rt_ref.shape
    held, own = layout.held, layout.own
    inner = held // own
    far, near = lax.axis_index("fo"), lax.axis_index("fi")
    pair = len(piece_refs)
    outer = parts // pair
    for i in range(pair):
        for o in range(outer):
            d = lax.rem(far - o + outer, outer) * pair + lax.rem(near - i + pair, pair)
            for k in range(3):
                for x in range(inner):
                    at = k * held + x * own
                    fld_ref[k, x * parts + d] = piece_refs[i][o, at : at + own]
            for slot in range(layout.slots - 3 * held):
                at = slot * layout.frac_rows
                ent_ref[d, at : at + layout.frac_rows, :] = piece_refs[i][o, 3 * held + slot]
    hot_rows(layout, ent_ref, rt_ref)
    for d in range(parts):
        cell = layout.entries(ent_ref, d, 0).astype(jnp.int32)
        col, half = cell % LANES, cell // LANES // rows
        for m in range(entries // LANES):
            at = slice(m * LANES, (m + 1) * LANES)
            iota_l = lax.broadcasted_iota(jnp.int32, (LANES, LANES), 0)
            for h in range(l_ref.shape[2] // LANES):
                mine = (iota_l == col[m : m + 1, :]) & (half[m : m + 1, :] == h)
                l_ref[d, at, h * LANES : (h + 1) * LANES] = jnp.where(mine, 1.0, 0.0).T.astype(BF16)
        tis = scatter_rows(split_high_low(layout.entries(ent_ref, d, 2), 3), rt_ref, l_ref, d)
        tis = tis.reshape(inner, *fld_ref.shape[2:])
        for x in range(inner):
            fld_ref[3, x * parts + d] = tis[x]


def arriving(o_ref, ent_ref, layout, parts):
    frac_rows, own = layout.frac_rows, layout.own
    inner = layout.held // own
    rows = layout.held * frac_rows
    export_rows = layout.export_rows
    iota = lax.broadcasted_iota(jnp.int32, (SUBS, LANES), 0)
    exported = []
    for d in range(parts):
        cell = layout.entries(ent_ref, d, 3).astype(jnp.int32)
        for e in range(export_rows):
            at = jnp.broadcast_to(cell[e : e + 1, :], (SUBS, LANES))
            row, col = at // LANES - iota, at % LANES
            found = [jnp.zeros((SUBS, LANES), F32) for _ in range(2)]
            for t in range(rows // SUBS):
                slot, r = t * SUBS // frac_rows, t * SUBS % frac_rows
                got = pick_lanes(o_ref[slot // own * parts + d, slot % own, r : r + SUBS, :], col)
                found[t % 2] = jnp.where(row == t * SUBS, got, found[t % 2])
            exported.append(jnp.sum(found[0] + found[1], axis=0, keepdims=True))
    out = []
    for d in range(parts):
        slot = layout.entries(ent_ref, d, 1).astype(jnp.int32)
        row, col = slot // LANES, slot % LANES
        x = jnp.zeros(slot.shape, F32)
        for t in range(parts * export_rows):
            if t // export_rows != d:
                got = pick_lanes(jnp.broadcast_to(exported[t], slot.shape), col)
                x = jnp.where(row == t, got, x)
        out.append(layout.entries(ent_ref, d, 2) * x)
    return out


def fine_kernel(layout, u_ref, s_ref, fld_ref, ent_ref, l_ref, o_ref, c_ref, rt_ref):
    total = o_ref.shape[0]
    own, J = layout.own, layout.J
    group = math.gcd(total, 8)
    hot_rows(layout, ent_ref, rt_ref)
    o_ref[...] = u_ref[:, 0] if len(u_ref.shape) == 5 else u_ref[...]

    fracs, inner = rt_ref.shape[0], layout.held // own

    def couple(d, values):
        c = scatter_rows(split_high_low(values, 2), rt_ref, l_ref, d)
        c = c.reshape(inner, *c_ref.shape[1:])
        for x in range(inner):
            c_ref[x * fracs + d] = c[x]

    def one_step(first):
        def blocks(ref, *index):
            return [parts_of(ref, (*index, pl.ds(first + b, 1)), 0, own, J) for b in range(group)]

        def sources(b):
            c = parts_of(c_ref, (pl.ds(first + b, 1),), 0, own, J)
            s = parts_of(s_ref, (pl.ds(first + b, 1), 1), 0, own, J)
            return [[s[k][j] + c[k][j] for j in range(J)] for k in range(own)]

        sto, per, lea, tis = (blocks(fld_ref, k) for k in range(4))
        out = implicit(blocks(o_ref), sto, per, lea, tis, sources, fine_size, SWEEPS)
        for b in range(group):
            put_parts(o_ref, (pl.ds(first + b, 1),), 0, out[b])

    def step(_, carry):
        values = arriving(o_ref, ent_ref, layout, fracs)
        for d in range(fracs):
            couple(d, values[d])

        def turn(g, carry):
            one_step(g * group)
            return carry

        return turn(0, carry) if total == group else lax.fori_loop(0, total // group, turn, carry)

    lax.fori_loop(0, FINE_STEPS, step, 0)


def chain_kernel(layout, kind, done, *refs):
    if kind == 0:
        p_ref, field_ref, s_ref, u_ref = refs
    elif kind == 1:
        p_ref, field_ref, s_ref, f_ref, old_ref, u_ref, g_ref = refs
    else:
        p_ref, field_ref, s_ref, f_ref, old_ref, out_ref, u_ref = refs
    slices = s_ref.shape[0]
    held, own, J = layout.held, layout.own, layout.J
    inner = held // own
    x = lax.axis_index("x")

    def at_source(n):
        return n % inner * (slices // inner) + n // inner

    def parts(ref, *index, first=0):
        return [[y[None] for y in part] for part in parts_of(ref, index, first, own, J)]

    def put(ref, index, value):
        put_parts(ref, index, 0, [[y[0] for y in part] for part in value])

    mine = x * (slices // inner) + lax.axis_index("fo") * layout.pair + lax.axis_index("fi")
    sto, per, lea = (parts(field_ref, k, mine) for k in range(3))
    at = (lambda n: (n, 0)) if kind == 0 else (lambda n: (n,))
    start = parts(p_ref, first=x * own)
    put(u_ref, at(0), start)
    if kind == 0:
        for n in range(slices):
            u_ref[n, 1] = s_ref[at_source(n)]

    def turn(n, u):
        sources = lambda b: parts(s_ref, at_source(n))
        (g,) = implicit([u], [sto], [per], [lea], None, sources, fine_size * FINE_STEPS, COARSE_SWEEPS)
        if kind:
            f = parts(f_ref, n)
            old = parts(old_ref, n + 1, 0) if len(old_ref.shape) == 5 else parts(old_ref, n)
            if kind == 1:
                put(g_ref, (n,), g)
            g = [[g[k][j] + (f[k][j] - old[k][j]) for j in range(J)] for k in range(own)]
        put(u_ref, at(n + 1), g)
        return g

    for n in range(done):
        start = parts(f_ref, n)
        put(u_ref, at(n + 1), start)
        if kind == 1:
            g_ref[n] = jnp.zeros(g_ref.shape[1:], F32)
    lax.fori_loop(done, slices - 1, turn, start)
    if kind == 1:
        g_ref[slices - 1] = jnp.zeros(g_ref.shape[1:], F32)
    if kind == 2:
        z = lax.axis_index("z")
        for k in range(inner):
            n = z * inner + lax.rem(x + k, inner)
            from_parts(out_ref, (k,), parts_of(u_ref, (n,), 0, own, J))


def gather_from(axis, a):
    n = lax.axis_size(axis)
    return [a] + [lax.ppermute(a, axis, [(i, (i + k) % n) for i in range(n)]) for k in range(1, n)]


def body(sizes, pressure0, storage, perm_base, leakoff, sources, export_cells, inter_local, trace_source, inter_trans, inter_count):
    groups, inner, outer, pair = sizes
    fracs = outer * pair
    slices = groups * inner
    held, frac_rows, _ = pressure0.shape
    own = held // inner
    plane = ("x", "fo", "fi")
    layout = Layout(held, own, pair, frac_rows, inter_local.size, export_cells.size)
    block = (own, frac_rows, LANES)
    plain = shape_of(slices, *block)

    lists = [a.reshape(-1, LANES) for a in (inter_local, trace_source, inter_trans, export_cells)]
    arrays = (storage, perm_base, leakoff, pressure0, sources, *lists, inter_count)
    packed, blocks, start = call(
        functools.partial(pack_kernel, layout),
        "pack",
        arrays,
        (shape_of(layout.slots, frac_rows, LANES), shape_of(inner, groups, *block), shape_of(*pressure0.shape)),
        [pltpu.VMEM(a.shape, a.dtype) for a in arrays[:-1]]
        + [pltpu.SMEM(inter_count.shape, jnp.int32), pltpu.SemaphoreType.DMA((len(arrays),))],
        [HBM] * len(arrays),
        56 * 2**20,
    )
    far = gather_from("fo", packed[None])
    own_sources = lax.all_to_all(blocks.reshape(plain.shape), ("x", "z"), 0, 0, tiled=True)
    pieces = gather_from("fi", jnp.concatenate(far, axis=0))
    hot = pltpu.VMEM((fracs, held * frac_rows // 2, inter_local.size), BF16)
    fld, ent, l = call(
        functools.partial(prep_kernel, layout),
        "prep",
        pieces,
        (
            shape_of(4, slices, *block),
            shape_of(fracs, (layout.slots - 3 * held) * frac_rows, LANES),
            shape_of(fracs, inter_local.size, 2 * LANES, dtype=BF16),
        ),
        [hot],
    )
    own_sources, fld, ent, l = lax.optimization_barrier((own_sources, fld, ent, l))

    base = (start, fld, own_sources)
    (u0,) = call(functools.partial(chain_kernel, layout, 0, 0), "chain0", base, (shape_of(slices, 2, *block),))
    b0 = lax.all_to_all(u0, plane, 0, 0, tiled=True)
    u, old = b0, u0
    for iteration in range(ITERS):
        (ends,) = call(
            functools.partial(fine_kernel, layout),
            "fine",
            (u, b0, fld, ent, l),
            (plain,),
            [pltpu.VMEM(plain.shape, F32), hot],
        )
        ends = lax.all_to_all(ends, plane, 0, 0, tiled=True)
        if iteration < ITERS - 1:
            states, old = call(functools.partial(chain_kernel, layout, 1, iteration + 1), "chain1", (*base, ends, old), (plain, plain))
            u = lax.all_to_all(states, plane, 0, 0, tiled=True)
    (mine,) = call(
        functools.partial(chain_kernel, layout, 2, ITERS),
        "chain2",
        (*base, ends, old),
        (shape_of(inner, *block),),
        [pltpu.VMEM(plain.shape, F32)],
    )
    x = lax.axis_index("x")
    got = [mine[0]] + [
        lax.ppermute(mine[k], "x", [(i, (i + k) % inner) for i in range(inner)]) for k in range(1, inner)
    ]
    return jnp.stack([lax.select_n((x - i) % inner, *got) if inner > 2 else jnp.where(x == i, got[0], got[-1]) for i in range(inner)]).reshape(1, held, frac_rows, LANES)


def solution(mesh):
    slices, fracs = mesh.shape["tm"], mesh.shape["frac"]
    inner = slices // fracs
    pair = math.gcd(fracs, 2)
    sizes = (slices // inner, inner, fracs // pair, pair)
    mesh = Mesh(mesh.devices.reshape(sizes), ("z", "x", "fo", "fi"))
    frac = P(("fo", "fi"))
    both = P(("z", "x"), ("fo", "fi"))
    return jax.shard_map(
        functools.partial(body, sizes),
        mesh=mesh,
        in_specs=(frac,) * 4 + (both,) + (frac,) * 5,
        out_specs=both,
        check_vma=False,
    )
```

```python
import functools
import math

import jax
import jax.numpy as jnp
from jax import lax
from jax.experimental import pallas as pl
from jax.experimental.pallas import tpu as pltpu
from jax.sharding import Mesh, PartitionSpec as P

FINE_STEPS = 4
SWEEPS = 8
COARSE_SWEEPS = 2
ITERS = 2

stress_factor = 0.15
fine_size = 0.25

LANES = 128
SUBS = 8
F32 = jnp.float32
BF16 = jnp.bfloat16
VMEM = pl.BlockSpec(memory_space=pltpu.VMEM)
HBM = pl.BlockSpec(memory_space=pltpu.HBM)


def shape_of(*dims, dtype=F32):
    return jax.ShapeDtypeStruct(dims, dtype)


def call(kernel, name, args, outs, scratch=(), specs=None, room=4 * 2**20):
    size = sum(math.prod(a.shape) * a.dtype.itemsize for a in (*args, *outs))
    return pl.pallas_call(
        kernel,
        out_shape=outs,
        in_specs=specs or [VMEM] * len(args),
        out_specs=(VMEM,) * len(outs),
        scratch_shapes=scratch,
        compiler_params=pltpu.CompilerParams(vmem_limit_bytes=room + size),
        name=name,
    )(*args)


def lane_roll(x, s):
    return pltpu.roll(x, s % LANES, axis=2)


def sub_roll(x, s):
    return pltpu.roll(x, s % SUBS, axis=1)


def coefficients(q, sto, per, lea, tis, step_size):
    M, J = len(q), len(q[0])
    shape = q[0][0].shape
    row = lax.broadcasted_iota(jnp.int32, shape, 1)
    col = lax.broadcasted_iota(jnp.int32, shape, 2) % (LANES // M)

    def each(f):
        return [[f(k, j) for j in range(J)] for k in range(M)]

    half = each(lambda k, j: (0.5 * per[k][j]) * jnp.exp(stress_factor * q[k][j]))
    down, up, right, left = neighbours(half, rolled(half))
    row_next = each(lambda k, j: half[k][j] + down[k][j])
    row_prev = each(lambda k, j: half[k][j] + up[k][j] if j == 0 else row_next[k][j - 1])
    col_next = each(lambda k, j: half[k][j] + right[k][j])
    col_prev = each(lambda k, j: half[k][j] + left[k][j] if k == 0 else col_next[k - 1][j])
    for k in range(M):
        row_next[k][J - 1] = jnp.where(row == SUBS - 1, 0.0, row_next[k][J - 1])
        row_prev[k][0] = jnp.where(row == 0, 0.0, row_prev[k][0])
    for j in range(J):
        col_next[M - 1][j] = jnp.where(col == LANES // M - 1, 0.0, col_next[M - 1][j])
        col_prev[0][j] = jnp.where(col == 0, 0.0, col_prev[0][j])

    def inverse(k, j):
        total = sto[k][j] * (1.0 / step_size) + lea[k][j]
        if tis is not None:
            total = total + tis[k][j]
        return 1.0 / ((total + (row_next[k][j] + row_prev[k][j])) + (col_next[k][j] + col_prev[k][j]))

    inv = each(inverse)
    return [inv] + [each(lambda k, j: t[k][j] * inv[k][j]) for t in (row_next, row_prev, col_next, col_prev)]


def rolled(v):
    return (
        [sub_roll(part[0], -1) for part in v],
        [sub_roll(part[-1], 1) for part in v],
        [lane_roll(x, -1) for x in v[0]],
        [lane_roll(x, 1) for x in v[-1]],
    )


def neighbours(v, edges):
    after, before, right, left = edges
    return (
        [part[1:] + [after[k]] for k, part in enumerate(v)],
        [[before[k]] + part[:-1] for k, part in enumerate(v)],
        v[1:] + [right],
        [left] + v[:-1],
    )


def implicit(q, sto, per, lea, tis, sources, step_size, sweeps):
    M, J = len(q[0]), len(q[0][0])
    grid = [(k, j) for k in range(M) for j in range(J)]
    blocks = range(len(q))
    known, edges, rhs = [], [], []
    for b in blocks:
        s = sources(b)
        known.append(coefficients(q[b], sto[b], per[b], lea[b], None if tis is None else tis[b], step_size))
        edges.append(rolled(q[b]))
        inv = known[b][0]
        rhs.append([[None] * J for _ in range(M)])
        for k, j in grid:
            rhs[b][k][j] = (sto[b][k][j] * (1.0 / step_size) * q[b][k][j] + s[k][j]) * inv[k][j]
    v = list(q)
    for sweep in range(sweeps):
        for b in blocks:
            _, a_rn, a_rp, a_cn, a_cp = known[b]
            down, up, right, left = neighbours(v[b], edges[b])
            new = [[None] * J for _ in range(M)]
            for k, j in grid:
                new[k][j] = (rhs[b][k][j] + a_rn[k][j] * down[k][j] + a_rp[k][j] * up[k][j]) + (
                    a_cn[k][j] * right[k][j] + a_cp[k][j] * left[k][j]
                )
            v[b] = new
            if sweep < sweeps - 1:
                edges[b] = rolled(new)
    return v


def parts_of(ref, index, first, M, J):
    return [[ref[(*index, first + k, pl.ds(j * SUBS, SUBS), slice(None))] for j in range(J)] for k in range(M)]


def put_parts(ref, index, first, parts):
    for k, part in enumerate(parts):
        for j, x in enumerate(part):
            ref[(*index, first + k, pl.ds(j * SUBS, SUBS), slice(None))] = x


def pick_lanes(x, index):
    return jnp.take_along_axis(x, index, axis=1, mode="promise_in_bounds")


def to_parts(ref, first, M, J):
    lane = lax.broadcasted_iota(jnp.int32, (SUBS, LANES), 1)
    width = LANES // M
    out = [[None] * J for _ in range(M)]
    for j in range(J):
        rows = [ref[first + f, pl.ds(j, SUBS, stride=J), :] for f in range(M)]
        for k in range(M):
            x = pick_lanes(rows[0], lane % width * M + k)
            for f in range(1, M):
                x = jnp.where(lane // width == f, pick_lanes(rows[f], lane % width * M + k), x)
            out[k][j] = x
    return out


def from_parts(ref, index, parts):
    lane = lax.broadcasted_iota(jnp.int32, (SUBS, LANES), 1)
    M, J = len(parts), len(parts[0])
    width = LANES // M
    for j in range(J):
        for f in range(M):
            x = pick_lanes(parts[0][j], lane // M + f * width)
            for k in range(1, M):
                x = jnp.where(lane % M == k, pick_lanes(parts[k][j], lane // M + f * width), x)
            ref[(*index, f, pl.ds(j, SUBS, stride=J), slice(None))] = x


def split_high_low(x, pieces):
    out = []
    for _ in range(pieces):
        part = x.astype(BF16).astype(F32)
        out.append(part)
        x = x - part
    return out


def scatter_rows(values, rt_ref, l_ref, d):
    rows, entries = rt_ref.shape[1:]
    pieces = []
    for value in values:
        cols = []
        for m in range(entries // LANES):
            row = jnp.broadcast_to(value[m : m + 1, :], (2 * SUBS, LANES)).astype(BF16)
            hot = rt_ref[d, :, m * LANES : (m + 1) * LANES].reshape(-1, 2 * SUBS, LANES)
            cols.append((hot * row[None]).reshape(rows, LANES))
        pieces.append(jnp.concatenate(cols, axis=1))
    both = jnp.dot(jnp.concatenate(pieces, axis=0), l_ref[d], preferred_element_type=F32)
    out = both[:rows]
    for i in range(1, len(values)):
        out = out + both[i * rows : (i + 1) * rows]
    return jnp.concatenate([out[:, h * LANES : (h + 1) * LANES] for h in range(out.shape[1] // LANES)], axis=0)


class Layout:
    def __init__(self, held, own, pair, frac_rows, entries, exports):
        self.held, self.own, self.pair, self.frac_rows = held, own, pair, frac_rows
        self.J = frac_rows // SUBS
        self.entry_rows = entries // LANES
        self.export_rows = exports // LANES
        padded = -(-self.export_rows // SUBS) * SUBS
        self.sizes = [self.entry_rows] * 3 + [self.export_rows]
        self.slots = 3 * held + -(-(3 * self.entry_rows + padded) // frac_rows)

    def place(self, cell):
        own, J = self.own, self.J
        f, row, col = cell // (self.frac_rows * LANES), cell // LANES % self.frac_rows, cell % LANES
        part = (f // own * own + col % own) * J + row % J
        return (part * SUBS + row // J) * LANES + f % own * (LANES // own) + col // own

    def entries(self, ref, d, kind):
        start = kind * self.entry_rows
        return ref[d, start : start + self.sizes[kind], :]

    def put(self, ref, kind, value):
        at, left, start = 0, self.sizes[kind], kind * self.entry_rows
        while left:
            n = min(left, SUBS)
            slot, r = 3 * self.held + start // self.frac_rows, start % self.frac_rows
            ref[slot, r : r + n, :] = value[at : at + n]
            at, start, left = at + n, start + n, left - n


def pack_kernel(layout, *refs):
    sources = refs[:10]
    out_ref, blocks_ref, p_ref = refs[10:13]
    held_refs, sems = refs[13:23], refs[23]
    held, own, J = layout.held, layout.own, layout.J
    copies = [pltpu.make_async_copy(a, b, sems.at[k]) for k, (a, b) in enumerate(zip(sources, held_refs))]
    for c in copies:
        c.start()
    out_ref[3 * held :] = jnp.zeros((layout.slots - 3 * held, *out_ref.shape[1:]), F32)
    for c in copies:
        c.wait()
    *fields, p, source, loc, trace, w, exp, count_ref = held_refs
    for first in range(0, held, own):
        for k, field in enumerate(fields):
            put_parts(out_ref, (), k * held + first, to_parts(field, first, own, J))
        put_parts(p_ref, (), first, to_parts(p, first, own, J))
        parts = to_parts(source.at[0], first, own, J)
        for z in range(blocks_ref.shape[1]):
            put_parts(blocks_ref, (first // own, z), 0, parts)
    shape = w.shape
    index = lax.broadcasted_iota(jnp.int32, shape, 0) * LANES + lax.broadcasted_iota(jnp.int32, shape, 1)
    layout.put(out_ref, 0, layout.place(loc[...]).astype(F32))
    layout.put(out_ref, 1, trace[...].astype(F32))
    layout.put(out_ref, 2, jnp.where(index < count_ref[0], w[...], 0.0))
    layout.put(out_ref, 3, layout.place(exp[...]).astype(F32))


def hot_rows(layout, ent_ref, rt_ref):
    parts, rows, entries = rt_ref.shape
    iota = lax.broadcasted_iota(jnp.int32, (rows, LANES), 0)
    for d in range(parts):
        row = layout.entries(ent_ref, d, 0).astype(jnp.int32) // LANES % rows
        for m in range(entries // LANES):
            at = slice(m * LANES, (m + 1) * LANES)
            rt_ref[d, :, at] = jnp.where(iota == row[m : m + 1, :], 1.0, 0.0).astype(BF16)


def prep_kernel(layout, *refs):
    *piece_refs, fld_ref, ent_ref, l_ref, rt_ref = refs
    parts, rows, entries = rt_ref.shape
    held, own = layout.held, layout.own
    inner = held // own
    far, near = lax.axis_index("fo"), lax.axis_index("fi")
    pair = len(piece_refs)
    outer = parts // pair
    for i in range(pair):
        for o in range(outer):
            d = lax.rem(far - o + outer, outer) * pair + lax.rem(near - i + pair, pair)
            for k in range(3):
                for x in range(inner):
                    at = k * held + x * own
                    fld_ref[k, x * parts + d] = piece_refs[i][o, at : at + own]
            for slot in range(layout.slots - 3 * held):
                at = slot * layout.frac_rows
                ent_ref[d, at : at + layout.frac_rows, :] = piece_refs[i][o, 3 * held + slot]
    hot_rows(layout, ent_ref, rt_ref)
    for d in range(parts):
        cell = layout.entries(ent_ref, d, 0).astype(jnp.int32)
        col, half = cell % LANES, cell // LANES // rows
        for m in range(entries // LANES):
            at = slice(m * LANES, (m + 1) * LANES)
            iota_l = lax.broadcasted_iota(jnp.int32, (LANES, LANES), 0)
            for h in range(l_ref.shape[2] // LANES):
                mine = (iota_l == col[m : m + 1, :]) & (half[m : m + 1, :] == h)
                l_ref[d, at, h * LANES : (h + 1) * LANES] = jnp.where(mine, 1.0, 0.0).T.astype(BF16)
        tis = scatter_rows(split_high_low(layout.entries(ent_ref, d, 2), 3), rt_ref, l_ref, d)
        tis = tis.reshape(inner, *fld_ref.shape[2:])
        for x in range(inner):
            fld_ref[3, x * parts + d] = tis[x]


def arriving(o_ref, ent_ref, layout, parts):
    frac_rows, own = layout.frac_rows, layout.own
    inner = layout.held // own
    rows = layout.held * frac_rows
    export_rows = layout.export_rows
    iota = lax.broadcasted_iota(jnp.int32, (SUBS, LANES), 0)
    exported = []
    for d in range(parts):
        cell = layout.entries(ent_ref, d, 3).astype(jnp.int32)
        for e in range(export_rows):
            at = jnp.broadcast_to(cell[e : e + 1, :], (SUBS, LANES))
            row, col = at // LANES - iota, at % LANES
            found = [jnp.zeros((SUBS, LANES), F32) for _ in range(4)]
            for t in range(rows // SUBS):
                slot, r = t * SUBS // frac_rows, t * SUBS % frac_rows
                got = pick_lanes(o_ref[slot // own * parts + d, slot % own, r : r + SUBS, :], col)
                found[t % 4] = jnp.where(row == t * SUBS, got, found[t % 4])
            every = (found[0] + found[1]) + (found[2] + found[3])
            for turn in (4, 2, 1):
                every = every + pltpu.roll(every, turn, axis=0)
            exported.append(every)
    out = []
    for d in range(parts):
        slot = layout.entries(ent_ref, d, 1).astype(jnp.int32)
        row, col = slot // LANES, slot % LANES
        x = [jnp.zeros(slot.shape, F32) for _ in range(2)]
        for t in range(parts * export_rows):
            if t // export_rows != d:
                got = pick_lanes(jnp.concatenate([exported[t]] * (slot.shape[0] // SUBS), axis=0), col)
                x[t % 2] = jnp.where(row == t, got, x[t % 2])
        x = x[0] + x[1]
        out.append(layout.entries(ent_ref, d, 2) * x)
    return out


def fine_kernel(layout, u_ref, s_ref, fld_ref, ent_ref, l_ref, o_ref, c_ref, rt_ref):
    total = o_ref.shape[0]
    own, J = layout.own, layout.J
    group = math.gcd(total, 8)
    hot_rows(layout, ent_ref, rt_ref)
    o_ref[...] = u_ref[:, 0] if len(u_ref.shape) == 5 else u_ref[...]

    fracs, inner = rt_ref.shape[0], layout.held // own

    def couple(d, values):
        c = scatter_rows(split_high_low(values, 2), rt_ref, l_ref, d)
        c = c.reshape(inner, *c_ref.shape[1:])
        for x in range(inner):
            c_ref[x * fracs + d] = c[x]

    def one_step(first):
        def blocks(ref, *index):
            return [parts_of(ref, (*index, pl.ds(first + b, 1)), 0, own, J) for b in range(group)]

        def sources(b):
            c = parts_of(c_ref, (pl.ds(first + b, 1),), 0, own, J)
            s = parts_of(s_ref, (pl.ds(first + b, 1), 1), 0, own, J)
            return [[s[k][j] + c[k][j] for j in range(J)] for k in range(own)]

        sto, per, lea, tis = (blocks(fld_ref, k) for k in range(4))
        out = implicit(blocks(o_ref), sto, per, lea, tis, sources, fine_size, SWEEPS)
        for b in range(group):
            put_parts(o_ref, (pl.ds(first + b, 1),), 0, out[b])

    def step(_, carry):
        values = arriving(o_ref, ent_ref, layout, fracs)
        for d in range(fracs):
            couple(d, values[d])

        def turn(g, carry):
            one_step(g * group)
            return carry

        return turn(0, carry) if total == group else lax.fori_loop(0, total // group, turn, carry)

    lax.fori_loop(0, FINE_STEPS, step, 0)


def chain_kernel(layout, kind, done, *refs):
    if kind == 0:
        p_ref, field_ref, s_ref, u_ref = refs
    elif kind == 1:
        p_ref, field_ref, s_ref, f_ref, old_ref, u_ref, g_ref = refs
    else:
        p_ref, field_ref, s_ref, f_ref, old_ref, out_ref, u_ref = refs
    slices = s_ref.shape[0]
    held, own, J = layout.held, layout.own, layout.J
    inner = held // own
    x = lax.axis_index("x")

    def at_source(n):
        return n % inner * (slices // inner) + n // inner

    def parts(ref, *index, first=0):
        return [[y[None] for y in part] for part in parts_of(ref, index, first, own, J)]

    def put(ref, index, value):
        put_parts(ref, index, 0, [[y[0] for y in part] for part in value])

    mine = x * (slices // inner) + lax.axis_index("fo") * layout.pair + lax.axis_index("fi")
    sto, per, lea = (parts(field_ref, k, mine) for k in range(3))
    at = (lambda n: (n, 0)) if kind == 0 else (lambda n: (n,))
    start = parts(p_ref, first=x * own)
    put(u_ref, at(0), start)
    if kind == 0:
        for n in range(slices):
            u_ref[n, 1] = s_ref[at_source(n)]

    def turn(n, u):
        sources = lambda b: parts(s_ref, at_source(n))
        (g,) = implicit([u], [sto], [per], [lea], None, sources, fine_size * FINE_STEPS, COARSE_SWEEPS)
        if kind:
            f = parts(f_ref, n)
            old = parts(old_ref, n + 1, 0) if len(old_ref.shape) == 5 else parts(old_ref, n)
            if kind == 1:
                put(g_ref, (n,), g)
            g = [[g[k][j] + (f[k][j] - old[k][j]) for j in range(J)] for k in range(own)]
        put(u_ref, at(n + 1), g)
        return g

    for n in range(done):
        start = parts(f_ref, n)
        put(u_ref, at(n + 1), start)
        if kind == 1:
            g_ref[n] = jnp.zeros(g_ref.shape[1:], F32)
    lax.fori_loop(done, slices - 1, turn, start)
    if kind == 1:
        g_ref[slices - 1] = jnp.zeros(g_ref.shape[1:], F32)
    if kind == 2:
        z = lax.axis_index("z")
        for k in range(inner):
            n = z * inner + lax.rem(x + k, inner)
            from_parts(out_ref, (k,), parts_of(u_ref, (n,), 0, own, J))


def gather_from(axis, a):
    n = lax.axis_size(axis)
    return [a] + [lax.ppermute(a, axis, [(i, (i + k) % n) for i in range(n)]) for k in range(1, n)]


def body(sizes, pressure0, storage, perm_base, leakoff, sources, export_cells, inter_local, trace_source, inter_trans, inter_count):
    groups, inner, outer, pair = sizes
    fracs = outer * pair
    slices = groups * inner
    held, frac_rows, _ = pressure0.shape
    own = held // inner
    plane = ("x", "fo", "fi")
    layout = Layout(held, own, pair, frac_rows, inter_local.size, export_cells.size)
    block = (own, frac_rows, LANES)
    plain = shape_of(slices, *block)

    lists = [a.reshape(-1, LANES) for a in (inter_local, trace_source, inter_trans, export_cells)]
    arrays = (storage, perm_base, leakoff, pressure0, sources, *lists, inter_count)
    packed, blocks, start = call(
        functools.partial(pack_kernel, layout),
        "pack",
        arrays,
        (shape_of(layout.slots, frac_rows, LANES), shape_of(inner, groups, *block), shape_of(*pressure0.shape)),
        [pltpu.VMEM(a.shape, a.dtype) for a in arrays[:-1]]
        + [pltpu.SMEM(inter_count.shape, jnp.int32), pltpu.SemaphoreType.DMA((len(arrays),))],
        [HBM] * len(arrays),
        56 * 2**20,
    )
    far = gather_from("fo", packed[None])
    own_sources = lax.all_to_all(blocks.reshape(plain.shape), ("x", "z"), 0, 0, tiled=True)
    pieces = gather_from("fi", jnp.concatenate(far, axis=0))
    hot = pltpu.VMEM((fracs, held * frac_rows // 2, inter_local.size), BF16)
    fld, ent, l = call(
        functools.partial(prep_kernel, layout),
        "prep",
        pieces,
        (
            shape_of(4, slices, *block),
            shape_of(fracs, (layout.slots - 3 * held) * frac_rows, LANES),
            shape_of(fracs, inter_local.size, 2 * LANES, dtype=BF16),
        ),
        [hot],
    )
    own_sources, fld, ent, l = lax.optimization_barrier((own_sources, fld, ent, l))

    base = (start, fld, own_sources)
    (u0,) = call(functools.partial(chain_kernel, layout, 0, 0), "chain0", base, (shape_of(slices, 2, *block),))
    b0 = lax.all_to_all(u0, plane, 0, 0, tiled=True)
    u, old = b0, u0
    for iteration in range(ITERS):
        (ends,) = call(
            functools.partial(fine_kernel, layout),
            "fine",
            (u, b0, fld, ent, l),
            (plain,),
            [pltpu.VMEM(plain.shape, F32), hot],
        )
        ends = lax.all_to_all(ends, plane, 0, 0, tiled=True)
        if iteration < ITERS - 1:
            states, old = call(functools.partial(chain_kernel, layout, 1, iteration + 1), "chain1", (*base, ends, old), (plain, plain))
            u = lax.all_to_all(states, plane, 0, 0, tiled=True)
    (mine,) = call(
        functools.partial(chain_kernel, layout, 2, ITERS),
        "chain2",
        (*base, ends, old),
        (shape_of(inner, *block),),
        [pltpu.VMEM(plain.shape, F32)],
    )
    x = lax.axis_index("x")
    got = [mine[0]] + [
        lax.ppermute(mine[k], "x", [(i, (i + k) % inner) for i in range(inner)]) for k in range(1, inner)
    ]
    return jnp.stack([lax.select_n((x - i) % inner, *got) if inner > 2 else jnp.where(x == i, got[0], got[-1]) for i in range(inner)]).reshape(1, held, frac_rows, LANES)


def solution(mesh):
    slices, fracs = mesh.shape["tm"], mesh.shape["frac"]
    inner = slices // fracs
    pair = math.gcd(fracs, 2)
    sizes = (slices // inner, inner, fracs // pair, pair)
    mesh = Mesh(mesh.devices.reshape(sizes), ("z", "x", "fo", "fi"))
    frac = P(("fo", "fi"))
    both = P(("z", "x"), ("fo", "fi"))
    return jax.shard_map(
        functools.partial(body, sizes),
        mesh=mesh,
        in_specs=(frac,) * 4 + (both,) + (frac,) * 5,
        out_specs=both,
        check_vma=False,
    )
```

```python
import functools
import math

import jax
import jax.numpy as jnp
from jax import lax
from jax.experimental import pallas as pl
from jax.experimental.pallas import tpu as pltpu
from jax.sharding import Mesh, PartitionSpec as P

FINE_STEPS = 4
SWEEPS = 8
COARSE_SWEEPS = 2
ITERS = 2

stress_factor = 0.15
fine_size = 0.25

LANES = 128
SUBS = 8
F32 = jnp.float32
BF16 = jnp.bfloat16
VMEM = pl.BlockSpec(memory_space=pltpu.VMEM)
HBM = pl.BlockSpec(memory_space=pltpu.HBM)


def shape_of(*dims, dtype=F32):
    return jax.ShapeDtypeStruct(dims, dtype)


def call(kernel, name, args, outs, scratch=(), specs=None, room=4 * 2**20):
    size = sum(math.prod(a.shape) * a.dtype.itemsize for a in (*args, *outs))
    return pl.pallas_call(
        kernel,
        out_shape=outs,
        in_specs=specs or [VMEM] * len(args),
        out_specs=(VMEM,) * len(outs),
        scratch_shapes=scratch,
        compiler_params=pltpu.CompilerParams(vmem_limit_bytes=room + size),
        name=name,
    )(*args)


def lane_roll(x, s):
    return pltpu.roll(x, s % LANES, axis=2)


def sub_roll(x, s):
    return pltpu.roll(x, s % SUBS, axis=1)


def coefficients(q, sto, per, lea, tis, step_size):
    M, J = len(q), len(q[0])
    shape = q[0][0].shape
    row = lax.broadcasted_iota(jnp.int32, shape, 1)
    col = lax.broadcasted_iota(jnp.int32, shape, 2) % (LANES // M)

    def each(f):
        return [[f(k, j) for j in range(J)] for k in range(M)]

    half = each(lambda k, j: (0.5 * per[k][j]) * jnp.exp(stress_factor * q[k][j]))
    down, up, right, left = neighbours(half, rolled(half))
    row_next = each(lambda k, j: half[k][j] + down[k][j])
    row_prev = each(lambda k, j: half[k][j] + up[k][j] if j == 0 else row_next[k][j - 1])
    col_next = each(lambda k, j: half[k][j] + right[k][j])
    col_prev = each(lambda k, j: half[k][j] + left[k][j] if k == 0 else col_next[k - 1][j])
    for k in range(M):
        row_next[k][J - 1] = jnp.where(row == SUBS - 1, 0.0, row_next[k][J - 1])
        row_prev[k][0] = jnp.where(row == 0, 0.0, row_prev[k][0])
    for j in range(J):
        col_next[M - 1][j] = jnp.where(col == LANES // M - 1, 0.0, col_next[M - 1][j])
        col_prev[0][j] = jnp.where(col == 0, 0.0, col_prev[0][j])

    def inverse(k, j):
        total = sto[k][j] * (1.0 / step_size) + lea[k][j]
        if tis is not None:
            total = total + tis[k][j]
        return 1.0 / ((total + (row_next[k][j] + row_prev[k][j])) + (col_next[k][j] + col_prev[k][j]))

    inv = each(inverse)
    return [inv] + [each(lambda k, j: t[k][j] * inv[k][j]) for t in (row_next, row_prev, col_next, col_prev)]


def rolled(v):
    return (
        [sub_roll(part[0], -1) for part in v],
        [sub_roll(part[-1], 1) for part in v],
        [lane_roll(x, -1) for x in v[0]],
        [lane_roll(x, 1) for x in v[-1]],
    )


def neighbours(v, edges):
    after, before, right, left = edges
    return (
        [part[1:] + [after[k]] for k, part in enumerate(v)],
        [[before[k]] + part[:-1] for k, part in enumerate(v)],
        v[1:] + [right],
        [left] + v[:-1],
    )


def implicit(q, sto, per, lea, tis, sources, step_size, sweeps):
    M, J = len(q[0]), len(q[0][0])
    grid = [(k, j) for k in range(M) for j in range(J)]
    blocks = range(len(q))
    known, edges, rhs = [], [], []
    for b in blocks:
        s = sources(b)
        known.append(coefficients(q[b], sto[b], per[b], lea[b], None if tis is None else tis[b], step_size))
        edges.append(rolled(q[b]))
        inv = known[b][0]
        rhs.append([[None] * J for _ in range(M)])
        for k, j in grid:
            rhs[b][k][j] = (sto[b][k][j] * (1.0 / step_size) * q[b][k][j] + s[k][j]) * inv[k][j]
    v = list(q)
    for sweep in range(sweeps):
        for b in blocks:
            _, a_rn, a_rp, a_cn, a_cp = known[b]
            down, up, right, left = neighbours(v[b], edges[b])
            new = [[None] * J for _ in range(M)]
            for k, j in grid:
                new[k][j] = (rhs[b][k][j] + a_rn[k][j] * down[k][j] + a_rp[k][j] * up[k][j]) + (
                    a_cn[k][j] * right[k][j] + a_cp[k][j] * left[k][j]
                )
            v[b] = new
            if sweep < sweeps - 1:
                edges[b] = rolled(new)
    return v


def parts_of(ref, index, first, M, J):
    return [[ref[(*index, first + k, pl.ds(j * SUBS, SUBS), slice(None))] for j in range(J)] for k in range(M)]


def put_parts(ref, index, first, parts):
    for k, part in enumerate(parts):
        for j, x in enumerate(part):
            ref[(*index, first + k, pl.ds(j * SUBS, SUBS), slice(None))] = x


def pick_lanes(x, index):
    return jnp.take_along_axis(x, index, axis=1, mode="promise_in_bounds")


def to_parts(ref, first, M, J):
    lane = lax.broadcasted_iota(jnp.int32, (SUBS, LANES), 1)
    width = LANES // M
    out = [[None] * J for _ in range(M)]
    for j in range(J):
        rows = [ref[first + f, pl.ds(j, SUBS, stride=J), :] for f in range(M)]
        for k in range(M):
            x = pick_lanes(rows[0], lane % width * M + k)
            for f in range(1, M):
                x = jnp.where(lane // width == f, pick_lanes(rows[f], lane % width * M + k), x)
            out[k][j] = x
    return out


def from_parts(ref, index, parts):
    lane = lax.broadcasted_iota(jnp.int32, (SUBS, LANES), 1)
    M, J = len(parts), len(parts[0])
    width = LANES // M
    for j in range(J):
        for f in range(M):
            x = pick_lanes(parts[0][j], lane // M + f * width)
            for k in range(1, M):
                x = jnp.where(lane % M == k, pick_lanes(parts[k][j], lane // M + f * width), x)
            ref[(*index, f, pl.ds(j, SUBS, stride=J), slice(None))] = x


def split_high_low(x, pieces):
    out = []
    for _ in range(pieces):
        part = x.astype(BF16).astype(F32)
        out.append(part)
        x = x - part
    return out


def scatter_rows(values, rt_ref, l_ref, d):
    rows, entries = rt_ref.shape[1:]
    pieces = []
    for value in values:
        cols = []
        for m in range(entries // LANES):
            row = jnp.broadcast_to(value[m : m + 1, :], (2 * SUBS, LANES)).astype(BF16)
            hot = rt_ref[d, :, m * LANES : (m + 1) * LANES].reshape(-1, 2 * SUBS, LANES)
            cols.append((hot * row[None]).reshape(rows, LANES))
        pieces.append(jnp.concatenate(cols, axis=1))
    both = jnp.dot(jnp.concatenate(pieces, axis=0), l_ref[d], preferred_element_type=F32)
    out = both[:rows]
    for i in range(1, len(values)):
        out = out + both[i * rows : (i + 1) * rows]
    return jnp.concatenate([out[:, h * LANES : (h + 1) * LANES] for h in range(out.shape[1] // LANES)], axis=0)


class Layout:
    def __init__(self, held, own, pair, frac_rows, entries, exports):
        self.held, self.own, self.pair, self.frac_rows = held, own, pair, frac_rows
        self.J = frac_rows // SUBS
        self.entry_rows = entries // LANES
        self.export_rows = exports // LANES
        padded = -(-self.export_rows // SUBS) * SUBS
        self.sizes = [self.entry_rows] * 3 + [self.export_rows]
        self.slots = 3 * held + -(-(3 * self.entry_rows + padded) // frac_rows)

    def place(self, cell):
        own, J = self.own, self.J
        f, row, col = cell // (self.frac_rows * LANES), cell // LANES % self.frac_rows, cell % LANES
        part = (f // own * own + col % own) * J + row % J
        return (part * SUBS + row // J) * LANES + f % own * (LANES // own) + col // own

    def entries(self, ref, d, kind):
        start = kind * self.entry_rows
        return ref[d, start : start + self.sizes[kind], :]

    def put(self, ref, kind, value):
        at, left, start = 0, self.sizes[kind], kind * self.entry_rows
        while left:
            n = min(left, SUBS)
            slot, r = 3 * self.held + start // self.frac_rows, start % self.frac_rows
            ref[slot, r : r + n, :] = value[at : at + n]
            at, start, left = at + n, start + n, left - n


def pack_kernel(layout, *refs):
    sources = refs[:10]
    out_ref, blocks_ref, p_ref = refs[10:13]
    held_refs, sems = refs[13:23], refs[23]
    held, own, J = layout.held, layout.own, layout.J
    copies = [pltpu.make_async_copy(a, b, sems.at[k]) for k, (a, b) in enumerate(zip(sources, held_refs))]
    for c in copies:
        c.start()
    out_ref[3 * held :] = jnp.zeros((layout.slots - 3 * held, *out_ref.shape[1:]), F32)
    for c in copies:
        c.wait()
    *fields, p, source, loc, trace, w, exp, count_ref = held_refs
    for first in range(0, held, own):
        for k, field in enumerate(fields):
            put_parts(out_ref, (), k * held + first, to_parts(field, first, own, J))
        put_parts(p_ref, (), first, to_parts(p, first, own, J))
        parts = to_parts(source.at[0], first, own, J)
        for z in range(blocks_ref.shape[1]):
            put_parts(blocks_ref, (first // own, z), 0, parts)
    shape = w.shape
    index = lax.broadcasted_iota(jnp.int32, shape, 0) * LANES + lax.broadcasted_iota(jnp.int32, shape, 1)
    layout.put(out_ref, 0, layout.place(loc[...]).astype(F32))
    layout.put(out_ref, 1, trace[...].astype(F32))
    layout.put(out_ref, 2, jnp.where(index < count_ref[0], w[...], 0.0))
    layout.put(out_ref, 3, layout.place(exp[...]).astype(F32))


def hot_rows(layout, ent_ref, rt_ref):
    parts, rows, entries = rt_ref.shape
    iota = lax.broadcasted_iota(jnp.int32, (rows, LANES), 0)
    for d in range(parts):
        row = layout.entries(ent_ref, d, 0).astype(jnp.int32) // LANES % rows
        for m in range(entries // LANES):
            at = slice(m * LANES, (m + 1) * LANES)
            rt_ref[d, :, at] = jnp.where(iota == row[m : m + 1, :], 1.0, 0.0).astype(BF16)


def prep_kernel(layout, *refs):
    *piece_refs, fld_ref, ent_ref, l_ref, rt_ref = refs
    parts, rows, entries = rt_ref.shape
    held, own = layout.held, layout.own
    inner = held // own
    far, near = lax.axis_index("fo"), lax.axis_index("fi")
    pair = len(piece_refs)
    outer = parts // pair
    for i in range(pair):
        for o in range(outer):
            d = lax.rem(far - o + outer, outer) * pair + lax.rem(near - i + pair, pair)
            for k in range(3):
                for x in range(inner):
                    at = k * held + x * own
                    fld_ref[k, x * parts + d] = piece_refs[i][o, at : at + own]
            for slot in range(layout.slots - 3 * held):
                at = slot * layout.frac_rows
                ent_ref[d, at : at + layout.frac_rows, :] = piece_refs[i][o, 3 * held + slot]
    hot_rows(layout, ent_ref, rt_ref)
    for d in range(parts):
        cell = layout.entries(ent_ref, d, 0).astype(jnp.int32)
        col, half = cell % LANES, cell // LANES // rows
        for m in range(entries // LANES):
            at = slice(m * LANES, (m + 1) * LANES)
            iota_l = lax.broadcasted_iota(jnp.int32, (LANES, LANES), 0)
            for h in range(l_ref.shape[2] // LANES):
                mine = (iota_l == col[m : m + 1, :]) & (half[m : m + 1, :] == h)
                l_ref[d, at, h * LANES : (h + 1) * LANES] = jnp.where(mine, 1.0, 0.0).T.astype(BF16)
        tis = scatter_rows(split_high_low(layout.entries(ent_ref, d, 2), 3), rt_ref, l_ref, d)
        tis = tis.reshape(inner, *fld_ref.shape[2:])
        for x in range(inner):
            fld_ref[3, x * parts + d] = tis[x]


def arriving(o_ref, ent_ref, layout, parts):
    frac_rows, own = layout.frac_rows, layout.own
    inner = layout.held // own
    rows = layout.held * frac_rows
    export_rows = layout.export_rows
    iota = lax.broadcasted_iota(jnp.int32, (SUBS, LANES), 0)
    exported = []
    for d in range(parts):
        cell = layout.entries(ent_ref, d, 3).astype(jnp.int32)
        for e in range(export_rows):
            at = jnp.broadcast_to(cell[e : e + 1, :], (SUBS, LANES))
            row, col = at // LANES - iota, at % LANES
            found = [jnp.zeros((SUBS, LANES), F32) for _ in range(2)]
            for t in range(rows // SUBS):
                slot, r = t * SUBS // frac_rows, t * SUBS % frac_rows
                got = pick_lanes(o_ref[slot // own * parts + d, slot % own, r : r + SUBS, :], col)
                found[t % 2] = jnp.where(row == t * SUBS, got, found[t % 2])
            exported.append(jnp.sum(found[0] + found[1], axis=0, keepdims=True))
    out = []
    for d in range(parts):
        slot = layout.entries(ent_ref, d, 1).astype(jnp.int32)
        row, col = slot // LANES, slot % LANES
        x = jnp.zeros(slot.shape, F32)
        for t in range(parts * export_rows):
            if t // export_rows != d:
                got = pick_lanes(jnp.broadcast_to(exported[t], slot.shape), col)
                x = jnp.where(row == t, got, x)
        out.append(layout.entries(ent_ref, d, 2) * x)
    return out


def fine_kernel(layout, u_ref, s_ref, fld_ref, ent_ref, l_ref, o_ref, c_ref, rt_ref):
    total = o_ref.shape[0]
    own, J = layout.own, layout.J
    group = math.gcd(total, 8)
    hot_rows(layout, ent_ref, rt_ref)
    o_ref[...] = u_ref[:, 0] if len(u_ref.shape) == 5 else u_ref[...]

    fracs, inner = rt_ref.shape[0], layout.held // own

    def couple(d, values):
        c = scatter_rows(split_high_low(values, 2), rt_ref, l_ref, d)
        c = c.reshape(inner, *c_ref.shape[1:])
        for x in range(inner):
            c_ref[x * fracs + d] = c[x]

    def one_step(first):
        def blocks(ref, *index):
            return [parts_of(ref, (*index, pl.ds(first + b, 1)), 0, own, J) for b in range(group)]

        def sources(b):
            c = parts_of(c_ref, (pl.ds(first + b, 1),), 0, own, J)
            s = parts_of(s_ref, (pl.ds(first + b, 1), 1), 0, own, J)
            return [[s[k][j] + c[k][j] for j in range(J)] for k in range(own)]

        sto, per, lea, tis = (blocks(fld_ref, k) for k in range(4))
        out = implicit(blocks(o_ref), sto, per, lea, tis, sources, fine_size, SWEEPS)
        for b in range(group):
            put_parts(o_ref, (pl.ds(first + b, 1),), 0, out[b])

    def step(_, carry):
        values = arriving(o_ref, ent_ref, layout, fracs)
        for d in range(fracs):
            couple(d, values[d])

        def turn(g, carry):
            one_step(g * group)
            return carry

        return turn(0, carry) if total == group else lax.fori_loop(0, total // group, turn, carry)

    lax.fori_loop(0, FINE_STEPS, step, 0)


def chain_kernel(layout, kind, done, *refs):
    if kind == 0:
        p_ref, field_ref, s_ref, u_ref = refs
    elif kind == 1:
        p_ref, field_ref, s_ref, f_ref, old_ref, u_ref, g_ref = refs
    else:
        p_ref, field_ref, s_ref, f_ref, old_ref, out_ref, u_ref = refs
    slices = s_ref.shape[0]
    held, own, J = layout.held, layout.own, layout.J
    inner = held // own
    x = lax.axis_index("x")

    def at_source(n):
        return n % inner * (slices // inner) + n // inner

    def parts(ref, *index, first=0):
        return [[y[None] for y in part] for part in parts_of(ref, index, first, own, J)]

    def put(ref, index, value):
        put_parts(ref, index, 0, [[y[0] for y in part] for part in value])

    mine = x * (slices // inner) + lax.axis_index("fo") * layout.pair + lax.axis_index("fi")
    sto, per, lea = (parts(field_ref, k, mine) for k in range(3))
    at = (lambda n: (n, 0)) if kind == 0 else (lambda n: (n,))
    start = parts(p_ref, first=x * own)
    put(u_ref, at(0), start)
    if kind == 0:
        for n in range(slices):
            u_ref[n, 1] = s_ref[at_source(n)]

    def turn(n, u):
        sources = lambda b: parts(s_ref, at_source(n))
        (g,) = implicit([u], [sto], [per], [lea], None, sources, fine_size * FINE_STEPS, COARSE_SWEEPS)
        if kind:
            f = parts(f_ref, n)
            old = parts(old_ref, n + 1, 0) if len(old_ref.shape) == 5 else parts(old_ref, n)
            if kind == 1:
                put(g_ref, (n,), g)
            g = [[g[k][j] + (f[k][j] - old[k][j]) for j in range(J)] for k in range(own)]
        put(u_ref, at(n + 1), g)
        return g

    for n in range(done):
        start = parts(f_ref, n)
        put(u_ref, at(n + 1), start)
        if kind == 1:
            g_ref[n] = jnp.zeros(g_ref.shape[1:], F32)
    lax.fori_loop(done, slices - 1, turn, start)
    if kind == 1:
        g_ref[slices - 1] = jnp.zeros(g_ref.shape[1:], F32)
    if kind == 2:
        z = lax.axis_index("z")
        for k in range(inner):
            n = z * inner + lax.rem(x + k, inner)
            from_parts(out_ref, (k,), parts_of(u_ref, (n,), 0, own, J))


def gather_from(axis, a):
    n = lax.axis_size(axis)
    return [a] + [lax.ppermute(a, axis, [(i, (i + k) % n) for i in range(n)]) for k in range(1, n)]


def body(sizes, pressure0, storage, perm_base, leakoff, sources, export_cells, inter_local, trace_source, inter_trans, inter_count):
    groups, inner, outer, pair = sizes
    fracs = outer * pair
    slices = groups * inner
    held, frac_rows, _ = pressure0.shape
    own = held // inner
    plane = ("x", "fo", "fi")
    layout = Layout(held, own, pair, frac_rows, inter_local.size, export_cells.size)
    block = (own, frac_rows, LANES)
    plain = shape_of(slices, *block)

    lists = [a.reshape(-1, LANES) for a in (inter_local, trace_source, inter_trans, export_cells)]
    arrays = (storage, perm_base, leakoff, pressure0, sources, *lists, inter_count)
    packed, blocks, start = call(
        functools.partial(pack_kernel, layout),
        "pack",
        arrays,
        (shape_of(layout.slots, frac_rows, LANES), shape_of(inner, groups, *block), shape_of(*pressure0.shape)),
        [pltpu.VMEM(a.shape, a.dtype) for a in arrays[:-1]]
        + [pltpu.SMEM(inter_count.shape, jnp.int32), pltpu.SemaphoreType.DMA((len(arrays),))],
        [HBM] * len(arrays),
        56 * 2**20,
    )
    far = gather_from("fo", packed[None])
    own_sources = lax.all_to_all(blocks.reshape(plain.shape), ("x", "z"), 0, 0, tiled=True)
    pieces = gather_from("fi", jnp.concatenate(far, axis=0))
    hot = pltpu.VMEM((fracs, held * frac_rows // 2, inter_local.size), BF16)
    fld, ent, l = call(
        functools.partial(prep_kernel, layout),
        "prep",
        pieces,
        (
            shape_of(4, slices, *block),
            shape_of(fracs, (layout.slots - 3 * held) * frac_rows, LANES),
            shape_of(fracs, inter_local.size, 2 * LANES, dtype=BF16),
        ),
        [hot],
    )
    own_sources, fld, ent, l = lax.optimization_barrier((own_sources, fld, ent, l))

    base = (start, fld, own_sources)
    (u0,) = call(functools.partial(chain_kernel, layout, 0, 0), "chain0", base, (shape_of(slices, 2, *block),))
    b0 = lax.all_to_all(u0, plane, 0, 0, tiled=True)
    u, old = b0, u0
    for iteration in range(ITERS):
        (ends,) = call(
            functools.partial(fine_kernel, layout),
            "fine",
            (u, b0, fld, ent, l),
            (plain,),
            [pltpu.VMEM(plain.shape, F32), hot],
        )
        ends = lax.all_to_all(ends, plane, 0, 0, tiled=True)
        if iteration < ITERS - 1:
            states, old = call(functools.partial(chain_kernel, layout, 1, iteration + 1), "chain1", (*base, ends, old), (plain, plain))
            u = lax.all_to_all(states, plane, 0, 0, tiled=True)
    (mine,) = call(
        functools.partial(chain_kernel, layout, 2, ITERS),
        "chain2",
        (*base, ends, old),
        (shape_of(inner, *block),),
        [pltpu.VMEM(plain.shape, F32)],
    )
    x = lax.axis_index("x")
    got = [mine[0]] + [
        lax.ppermute(mine[k], "x", [(i, (i + k) % inner) for i in range(inner)]) for k in range(1, inner)
    ]
    out = jnp.zeros((held, frac_rows, LANES), F32)
    for k in range(inner):
        out = lax.dynamic_update_slice_in_dim(out, got[k], (x - k) % inner * own, 0)
    return out[None]


def solution(mesh):
    slices, fracs = mesh.shape["tm"], mesh.shape["frac"]
    inner = slices // fracs
    pair = math.gcd(fracs, 2)
    sizes = (slices // inner, inner, fracs // pair, pair)
    mesh = Mesh(mesh.devices.reshape(sizes), ("z", "x", "fo", "fi"))
    frac = P(("fo", "fi"))
    both = P(("z", "x"), ("fo", "fi"))
    return jax.shard_map(
        functools.partial(body, sizes),
        mesh=mesh,
        in_specs=(frac,) * 4 + (both,) + (frac,) * 5,
        out_specs=both,
        check_vma=False,
    )
```
